512 devices in a mesh: seq: 64 (over x_lo, z, core), exp: 8 (over x_hi, y).
Axes of the slice: x: 4 (x_hi: 2, x_lo: 2; x = x_hi * 2 + x_lo), y: 4, z: 16, core: 2. Of those that a mesh axis runs over, the one named last changes fastest.
Arguments:
- tokens: bfloat16 [16384, 2048], P('seq', 'exp'), may hold values from -11 to 11
- cotangent: bfloat16 [16384, 2048], P('seq', 'exp'), may hold values from -6 to 6
- slot_keys: bfloat16 [2048, 16], P(None, 'exp'), may hold values from -1 to 1
- expert_in: bfloat16 [16, 2048, 8192], P('exp', None, 'seq'), may hold values from -0.125 to 0.125
- expert_out: bfloat16 [16, 8192, 2048], P('exp', 'seq'), may hold values from -0.0625 to 0.0625
Outputs:
- token_grad: bfloat16 [16384, 2048], P('seq', 'exp')
- key_grad: float32 [2048, 16], P('seq', 'exp')
- in_grad: bfloat16 [16, 2048, 8192], P('exp', None, 'seq')
- out_grad: bfloat16 [16, 8192, 2048], P('exp', 'seq')
The draws below stay inside these ranges and needn't reach their ends.
All inputs are finite; a program needn't handle non-finite values.
Results may differ from the reference program's by a relative error of at most 0.018.
Values may be sent and summed in bfloat16 or wider, within the bound.
A program may use at most 64 MiB of HBM per device.

```python
import jax
import jax.numpy as jnp
from jax import lax

D = 2048
FF = 8192
TOKENS = 16384
SLOTS = 16


def key_values(key):
    normal_key = jax.random.fold_in(key, 11)
    gauss = jax.random.truncated_normal(normal_key, -6.0, 6.0, (D, SLOTS), jnp.float32)
    return gauss / jnp.sqrt(jnp.float32(D))


def draw_slot_keys(key, part):
    values = key_values(key)
    return jnp.clip(values, -1.0, 1.0).astype(jnp.bfloat16)


def draw_tokens(key, part):
    key = jax.random.fold_in(key, 5)
    first_key, second_key = jax.random.split(key, 2)
    position = jnp.arange(TOKENS, dtype=jnp.float32) / jnp.float32(TOKENS)
    rising = 0.5 * jnp.power(3.0, position)
    bound = jnp.float32(10 + 4000 // D)
    base = jax.random.truncated_normal(first_key, -4.0, 4.0, (TOKENS, D), jnp.float32)
    rough = jax.random.uniform(second_key, (TOKENS, 1), jnp.float32, 0.7, 1.4)
    values = base * rising[:, None] * rough
    return jnp.clip(values, -bound, bound).astype(jnp.bfloat16)


def steps_of(key, extent, shards, least, top_value):
    gain, own = 1.0, jax.random.fold_in(key, 6)
    for dim, parts in shards:
        steps = jnp.exp(jax.random.uniform(jax.random.fold_in(own, dim), (parts,), jnp.float32, least / len(shards), top_value / len(shards)))
        gain = gain * jnp.repeat(steps, extent[dim] // parts).reshape([-1 if axis == dim else 1 for axis in range(len(extent))])
    return gain


def normal_values(stream_key, dims, scale, most, pieces=(), kind=jnp.bfloat16):
    gain = steps_of(stream_key, dims, pieces, -0.22, 0.18) if pieces else 1.0
    entries = jax.random.normal(stream_key, dims, jnp.float32) * scale * gain
    return jnp.minimum(jnp.maximum(entries, -most), most).astype(kind)


def setup_inputs(seed: int = 0) -> dict:
    seeds = jax.random.split(jax.random.key(seed), 6)
    return {
        "tokens": draw_tokens(jax.random.fold_in(seeds[5], 71), 0),
        "cotangent": normal_values(seeds[1], (TOKENS, D), 1.0, 6.0, ((0, 64), (1, 8))),
        "slot_keys": draw_slot_keys(jax.random.fold_in(seeds[5], 71), 0),
        "expert_in": normal_values(seeds[3], (SLOTS, D, FF), D ** -0.5, 0.125, ((0, 8), (2, 64))),
        "expert_out": normal_values(seeds[4], (SLOTS, FF, D), FF ** -0.5, 0.0625, ((0, 8), (1, 64))),
    }


def gelu_tanh(values):
    return jax.nn.gelu(values, approximate=True)

def reference(tokens, cotangent, slot_keys, expert_in, expert_out):
    logits = jnp.dot(tokens, slot_keys, preferred_element_type=jnp.float32)
    col_peak = lax.optimization_barrier(jnp.max(logits, axis=0))
    col_exp = jnp.exp(logits - col_peak[None, :])
    dispatch = col_exp / lax.optimization_barrier(jnp.sum(col_exp, axis=0))[None, :]
    row_peak = lax.optimization_barrier(jnp.max(logits, axis=1))
    row_exp = jnp.exp(logits - row_peak[:, None])
    combine = row_exp / lax.optimization_barrier(jnp.sum(row_exp, axis=1))[:, None]
    dispatch_b = dispatch.astype(jnp.bfloat16)
    combine_b = combine.astype(jnp.bfloat16)
    slot_in = jnp.dot(dispatch_b.T, tokens, preferred_element_type=jnp.float32).astype(jnp.bfloat16)

    def expert_forward(index):
        pre_row = jnp.dot(slot_in[index][None, :], expert_in[index], preferred_element_type=jnp.float32)[0]
        hidden_row = gelu_tanh(pre_row).astype(jnp.bfloat16)
        out_row = jnp.dot(hidden_row[None, :], expert_out[index], preferred_element_type=jnp.float32)[0]
        return (pre_row, hidden_row, out_row.astype(jnp.bfloat16))
    pre, hidden, slot_out = lax.map(expert_forward, jnp.arange(SLOTS, dtype=jnp.int32))
    grad_combine = jnp.dot(cotangent, slot_out.T, preferred_element_type=jnp.float32)
    combine_row = lax.optimization_barrier(jnp.sum(combine * grad_combine, axis=1))
    logit_comb = combine * (grad_combine - combine_row[:, None])
    grad_slot_out = jnp.dot(combine_b.T, cotangent, preferred_element_type=jnp.float32).astype(jnp.bfloat16)

    def expert_backward(index):
        out_block = jnp.dot(hidden[index][:, None], grad_slot_out[index][None, :], preferred_element_type=jnp.float32)
        grad_hidden = jnp.dot(grad_slot_out[index][None, :], expert_out[index].T, preferred_element_type=jnp.float32)[0]
        unused, back = jax.vjp(gelu_tanh, pre[index])
        grad_pre = back(grad_hidden)[0].astype(jnp.bfloat16)
        in_block = jnp.dot(slot_in[index][:, None], grad_pre[None, :], preferred_element_type=jnp.float32)
        grad_in_row = jnp.dot(grad_pre[None, :], expert_in[index].T, preferred_element_type=jnp.float32)[0]
        return (in_block.astype(jnp.bfloat16), out_block.astype(jnp.bfloat16), grad_in_row.astype(jnp.bfloat16))
    in_grad, out_grad, grad_slot_in = lax.map(expert_backward, jnp.arange(SLOTS, dtype=jnp.int32))
    grad_dispatch = jnp.dot(tokens, grad_slot_in.T, preferred_element_type=jnp.float32)
    dispatch_col = lax.optimization_barrier(jnp.sum(dispatch * grad_dispatch, axis=0))
    logit_disp = dispatch * (grad_dispatch - dispatch_col[None, :])
    grad_logits = (logit_disp + logit_comb).astype(jnp.bfloat16)
    token_grad = jnp.dot(dispatch_b, grad_slot_in, preferred_element_type=jnp.float32)
    token_grad = token_grad + jnp.dot(grad_logits, slot_keys.T, preferred_element_type=jnp.float32)
    key_grad = jnp.dot(tokens.T, grad_logits, preferred_element_type=jnp.float32)
    return (token_grad.astype(jnp.bfloat16), key_grad, in_grad, out_grad)
```

```python
import jax
import jax.numpy as jnp
from jax import lax
from jax.experimental import pallas as pl
from jax.experimental.pallas import tpu as pltpu
from jax.sharding import PartitionSpec as P

MESH = pl.DeviceIdType.MESH
F32, BF16 = jnp.float32, jnp.bfloat16
ROOT_2_PI, CUBE = 0.7978845608, 0.044715


def dot(lhs, rhs, lhs_dim, rhs_dim):
    return lax.dot_general(
        lhs, rhs, (((lhs_dim,), (rhs_dim,)), ((), ())), preferred_element_type=F32
    )


def kernel(
    keys_ref, tokens_hbm, cotan_hbm, win_hbm, wout_hbm,
    token_grad_ref, key_row_ref, in_grad_hbm, out_grad_hbm,
    tok, cot, win, wout, in_grad, out_grad,
    key_buf, log_src, log_buf, c1_src, c1_buf, z_src, z_buf, d_buf,
    e1_src, e1_buf, e2_src, e2_buf, e3_src, e3_buf, g_src, g_buf, h_src, h_buf,
    gsi_rows, lse_rows, load_sem, store_sem, send_sem, recv_sem,
):
    i, e = lax.axis_index("seq"), lax.axis_index("exp")
    x_lo, z, core = i // 32, (i // 2) % 16, i % 2
    q = x_lo * 2 + core

    def seq_of(quarter, z_at):
        return (quarter // 2) * 32 + z_at * 2 + quarter % 2

    loads = [
        pltpu.make_async_copy(src, dst, load_sem.at[n])
        for n, (src, dst) in enumerate(
            ((tokens_hbm, tok), (cotan_hbm, cot), (win_hbm, win), (wout_hbm, wout))
        )
    ]
    for load in loads:
        load.start()

    barrier = pltpu.get_barrier_semaphore()
    for k in range(1, 8):
        pl.semaphore_signal(barrier, 1, device_id=(i, (e + k) % 8), device_id_type=MESH)
    for k in range(1, 64):
        pl.semaphore_signal(barrier, 1, device_id=((i + k) % 64, e), device_id_type=MESH)
    pl.semaphore_wait(barrier, 70)

    def send(phase, src, dst, seq_at, exp_at):
        pltpu.make_async_remote_copy(
            src, dst, send_sem.at[phase], recv_sem.at[phase],
            device_id=(seq_at, exp_at), device_id_type=MESH,
        ).start()

    def keep(phase, src, dst):
        pltpu.make_async_copy(src, dst, recv_sem.at[phase]).start()

    def arrive(phase, ref):
        pltpu.make_async_copy(ref, ref, recv_sem.at[phase]).wait()

    def sent(phase, ref):
        pltpu.make_async_copy(ref, ref, send_sem.at[phase]).wait()

    for k in range(1, 8):
        to = (e + k) % 8
        send(0, keys_ref.at[to], key_buf.at[e], i, to)
    key_buf[e] = keys_ref[e]
    loads[0].wait()
    arrive(0, key_buf.at[pl.ds(0, 7)])
    keys = key_buf[...].reshape(16, 256).astype(BF16)

    log_src[...] = dot(keys, tok[...], 1, 1)
    for k in range(1, 8):
        to = (e + k) % 8
        send(1, log_src, log_buf.at[e], i, to)
    log_buf[e] = log_src[...]
    loads[1].wait()
    arrive(1, log_buf.at[pl.ds(0, 7)])
    logits = log_buf[0]
    for k in range(1, 8):
        logits = logits + log_buf[k]

    peak = jnp.max(logits, axis=1, keepdims=True)
    weight_b = jnp.exp(logits - peak).astype(BF16)
    weight = weight_b.astype(F32)
    total = jnp.sum(weight, axis=1, keepdims=True)
    lse = peak + jnp.log(total)
    row_exp = jnp.exp(logits - jnp.max(logits, axis=0, keepdims=True))
    combine = row_exp / jnp.sum(row_exp, axis=0, keepdims=True)

    slot_part = dot(weight_b, tok[...], 1, 0) / total
    gout_part = dot(combine.astype(BF16), cot[...], 1, 0) * 16.0
    lse_wide = jnp.broadcast_to(lse, (16, 256))
    for b in range(8):
        c1_src[b, 0:2] = slot_part[2 * b : 2 * b + 2]
        c1_src[b, 2:4] = gout_part[2 * b : 2 * b + 2]
        c1_src[b, 4:6] = lse_wide[2 * b : 2 * b + 2]
        c1_src[b, 6:8] = jnp.zeros((2, 256), F32)
    home = seq_of(e // 2, z)
    c1_self = home == i
    for k in range(8):
        to = (e + k) % 8
        if k == 0:
            @pl.when(c1_self)
            def _():
                keep(2, c1_src.at[to], c1_buf.at[e % 2, q])

            @pl.when(jnp.logical_not(c1_self))
            def _():
                send(2, c1_src.at[to], c1_buf.at[e % 2, q], home, to)
        else:
            send(2, c1_src.at[to], c1_buf.at[e % 2, q], home, to)
    arrive(2, c1_buf)
    for h in range(2):
        part = [c1_buf[h, n] for n in range(4)]
        top = part[0][4:6]
        for n in range(1, 4):
            top = jnp.maximum(top, part[n][4:6])
        scale = [jnp.exp(part[n][4:6] - top) for n in range(4)]
        norm = scale[0] + scale[1] + scale[2] + scale[3]
        acc = part[0][0:2] * scale[0]
        gout = part[0][2:4]
        for n in range(1, 4):
            acc = acc + part[n][0:2] * scale[n]
            gout = gout + part[n][2:4]
        z_src[4 * h : 4 * h + 2, 0:256] = acc / norm
        z_src[4 * h + 2 : 4 * h + 4, 0:256] = gout
        z_src[4 * h : 4 * h + 2, 256:384] = (top + jnp.log(norm))[:, 0:128]
        z_src[4 * h + 2 : 4 * h + 4, 256:384] = jnp.zeros((2, 128), F32)

    for k in range(1, 16):
        send(3, z_src, z_buf.at[z], seq_of(q, (z + k) % 16), e)
    z_buf[z] = z_src[...]
    arrive(3, z_buf.at[pl.ds(0, 15)])
    top = z_buf[0, :, 256:384]
    for n in range(1, 16):
        top = jnp.maximum(top, z_buf[n, :, 256:384])
    norm = jnp.zeros((8, 128), F32)
    low, high = jnp.zeros((8, 128), F32), jnp.zeros((8, 128), F32)
    for n in range(16):
        scale = jnp.exp(z_buf[n, :, 256:384] - top)
        norm = norm + scale
        low = low + scale * z_buf[n, :, 0:128]
        high = high + scale * z_buf[n, :, 128:256]
    chunk = jnp.concatenate([low / norm, high / norm], axis=1)
    lse_all = top + jnp.log(norm)

    d_buf[q] = chunk
    for k in range(1, 4):
        send(4, d_buf.at[q], d_buf.at[q], seq_of((q + k) % 4, z), e)
    loads[2].wait()
    loads[3].wait()
    arrive(4, d_buf.at[pl.ds(0, 3)])

    vec = [d_buf[n].astype(BF16) for n in range(4)]
    pre, grad_hidden = [], []
    for s in range(2):
        total_p, total_g = [None, None], [None, None]
        for n in range(4):
            for h in range(2):
                at = n * 512 + h * 256
                p = dot(vec[n], win[s, at : at + 256, :], 1, 0)
                g = dot(vec[n], wout[s, :, at : at + 256], 1, 1)
                total_p[h] = p if total_p[h] is None else total_p[h] + p
                total_g[h] = g if total_g[h] is None else total_g[h] + g
        pre.append(total_p[0][s : s + 1] + total_p[1][4 + s : 5 + s])
        grad_hidden.append(total_g[0][2 + s : 3 + s] + total_g[1][6 + s : 7 + s])
    pre = jnp.concatenate(pre, axis=0)
    grad_hidden = jnp.concatenate(grad_hidden, axis=0)
    tanh = jnp.tanh(ROOT_2_PI * (pre + CUBE * pre * pre * pre))
    hidden = 0.5 * pre * (1.0 + tanh)
    slope = 0.5 * (1.0 + tanh) + 0.5 * pre * (1.0 - tanh * tanh) * ROOT_2_PI * (
        1.0 + 3.0 * CUBE * pre * pre
    )
    grad_pre = grad_hidden * slope
    zero = jnp.zeros((1, 128), F32)
    pad = jnp.zeros((6, 128), F32)
    hidden_b = [
        jnp.concatenate([hidden[0:1], zero, pad], axis=0).astype(BF16),
        jnp.concatenate([zero, hidden[1:2], pad], axis=0).astype(BF16),
    ]
    grad_pre_b = [
        jnp.concatenate([grad_pre[0:1], zero, pad], axis=0).astype(BF16),
        jnp.concatenate([zero, grad_pre[1:2], pad], axis=0).astype(BF16),
    ]

    for n in range(4):
        for h in range(2):
            at = n * 512 + h * 256
            out = dot(hidden_b[0], wout[0, :, at : at + 256], 1, 0) + dot(
                hidden_b[1], wout[1, :, at : at + 256], 1, 0
            )
            gin = dot(grad_pre_b[0], win[0, at : at + 256, :], 1, 1) + dot(
                grad_pre_b[1], win[1, at : at + 256, :], 1, 1
            )
            e1_src[n, 4 * h : 4 * h + 2, :] = gin[0:2]
            e1_src[n, 4 * h + 2 : 4 * h + 4, :] = out[0:2]
    for k in range(1, 4):
        to = (q + k) % 4
        send(5, e1_src.at[to], e1_buf.at[q], seq_of(to, z), e)
    e1_buf[q] = e1_src[q]
    arrive(5, e1_buf.at[pl.ds(0, 3)])
    e2_src[...] = (e1_buf[0] + e1_buf[1]) + (e1_buf[2] + e1_buf[3])
    for k in range(1, 16):
        send(6, e2_src, e2_buf.at[z], seq_of(q, (z + k) % 16), e)
    e2_buf[z] = e2_src[...]

    for s in range(2):
        for n in range(4):
            for h in range(2):
                at = n * 512 + h * 256
                mask_in = lax.broadcasted_iota(jnp.int32, (8, 128), 0) == 4 * h + s
                rows_in = jnp.where(mask_in, grad_pre[s : s + 1], 0.0).astype(BF16)
                in_grad[s, at : at + 256, :] = dot(vec[n], rows_in, 0, 0).astype(BF16)
                mask_out = lax.broadcasted_iota(jnp.int32, (8, 128), 0) == 4 * h + 2 + s
                rows_out = jnp.where(mask_out, hidden[s : s + 1], 0.0).astype(BF16)
                out_grad[s, :, at : at + 256] = dot(rows_out, vec[n], 0, 0).astype(BF16)
    stores = [
        pltpu.make_async_copy(in_grad, in_grad_hbm, store_sem.at[0]),
        pltpu.make_async_copy(out_grad, out_grad_hbm, store_sem.at[1]),
    ]
    for store in stores:
        store.start()

    arrive(6, e2_buf.at[pl.ds(0, 15)])
    full = e2_buf[0]
    for n in range(1, 16):
        full = full + e2_buf[n]
    full = full.astype(BF16).astype(F32)
    inner = jnp.sum(full * chunk, axis=1, keepdims=True)
    inner = jnp.broadcast_to(inner, (8, 256))
    lse_pair = jnp.concatenate([lse_all, lse_all], axis=1)
    for h in range(2):
        e3_src[h, 0:4] = full[4 * h : 4 * h + 4]
        e3_src[h, 4:6] = lse_pair[0:2]
        e3_src[h, 6:8] = inner[4 * h : 4 * h + 2]

    for k in range(4):
        to_q = (q + k) % 4
        for h in range(2):
            to_e = 2 * q + h
            if k == 0:
                @pl.when(to_e == e)
                def _():
                    keep(7, e3_src.at[h], e3_buf.at[e])

                @pl.when(to_e != e)
                def _():
                    send(7, e3_src.at[h], e3_buf.at[e], seq_of(to_q, z), to_e)
            else:
                send(7, e3_src.at[h], e3_buf.at[e], seq_of(to_q, z), to_e)
    arrive(7, e3_buf)
    stack = e3_buf[...].reshape(64, 256).astype(BF16)
    by_cot = dot(stack, cot[...], 1, 1)
    by_tok = dot(stack, tok[...], 1, 1)
    for b in range(8):
        g_src[2 * b : 2 * b + 2] = by_tok[8 * b : 8 * b + 2] - e3_buf[b, 6:8]
        g_src[16 + 2 * b : 18 + 2 * b] = by_cot[8 * b + 2 : 8 * b + 4]
    for k in range(1, 8):
        to = (e + k) % 8
        send(8, g_src, g_buf.at[e], i, to)
    g_buf[e] = g_src[...]
    for b in range(8):
        gsi_rows[2 * b : 2 * b + 2] = e3_buf[b, 0:2]
        lse_rows[2 * b : 2 * b + 2] = e3_buf[b, 4:6]
    dispatch = weight * (jnp.exp(lse - lse_rows[...]) / total)
    arrive(8, g_buf.at[pl.ds(0, 7)])
    grads = g_buf[0]
    for k in range(1, 8):
        grads = grads + g_buf[k]
    grad_dispatch, grad_combine = grads[0:16], grads[16:32]
    combine_row = jnp.sum(combine * grad_combine, axis=0, keepdims=True)
    grad_logits = dispatch * grad_dispatch + combine * (grad_combine - combine_row)
    grad_logits_b = grad_logits.astype(BF16)

    key_part = dot(grad_logits_b, tok[...], 1, 0)
    lane = lax.broadcasted_iota(jnp.int32, (16, 128), 1)
    for a in range(8):
        own = (key_part if a == 0 else pltpu.roll(key_part, 256 - 32 * a, 1))[:, 0:128]
        odd = pltpu.roll(pltpu.roll(own, 32, 1), 15, 0)
        row = jnp.where(lane < 32, own, odd)
        for b in range(8):
            h_src[a * 8 + b] = row[2 * b : 2 * b + 1]
    h_here = i // 8 == e

    for k in range(8):
        for m in range(8):
            a, b = (i + k) % 8, (e + m) % 8
            to = 8 * e + a
            if k == 0 and m == 0:
                @pl.when(h_here)
                def _():
                    keep(9, h_src.at[a * 8 + b], h_buf.at[i])

                @pl.when(jnp.logical_not(h_here))
                def _():
                    send(9, h_src.at[a * 8 + b], h_buf.at[i], to, b)
            else:
                send(9, h_src.at[a * 8 + b], h_buf.at[i], to, b)

    left = jnp.concatenate([dispatch.astype(BF16), grad_logits_b], axis=0)
    right = jnp.concatenate([gsi_rows[...].astype(BF16), keys], axis=0)
    token_grad_ref[...] = dot(left, right, 0, 0).astype(BF16)
    arrive(9, h_buf)
    rows = h_buf[0]
    for n in range(1, 64):
        rows = rows + h_buf[n]
    key_row_ref[...] = rows

    for store in stores:
        store.wait()
    sent(0, key_buf.at[pl.ds(0, 7)])
    sent(1, log_buf.at[pl.ds(0, 7)])

    @pl.when(c1_self)
    def _():
        sent(2, c1_src.at[pl.ds(0, 7)])

    @pl.when(jnp.logical_not(c1_self))
    def _():
        sent(2, c1_src)

    sent(3, z_buf.at[pl.ds(0, 15)])
    sent(4, d_buf.at[pl.ds(0, 3)])
    sent(5, e1_buf.at[pl.ds(0, 3)])
    sent(6, e2_buf.at[pl.ds(0, 15)])

    @pl.when(e // 2 == q)
    def _():
        sent(7, e3_buf.at[pl.ds(0, 7)])

    @pl.when(e // 2 != q)
    def _():
        sent(7, e3_buf)

    sent(8, g_buf.at[pl.ds(0, 7)])

    @pl.when(h_here)
    def _():
        sent(9, h_buf.at[pl.ds(0, 63)])

    @pl.when(jnp.logical_not(h_here))
    def _():
        sent(9, h_buf)


def per_device(tokens, cotangent, slot_keys, expert_in, expert_out):
    keys = slot_keys.astype(F32).T.reshape(2, 8, 256).transpose(1, 0, 2)
    any_space = pl.BlockSpec(memory_space=pl.ANY)
    vmem = pl.BlockSpec(memory_space=pltpu.VMEM)
    buf = pltpu.VMEM
    token_grad, key_row, in_grad, out_grad = pl.pallas_call(
        kernel,
        out_shape=(
            jax.ShapeDtypeStruct((256, 256), BF16),
            jax.ShapeDtypeStruct((1, 128), F32),
            jax.ShapeDtypeStruct((2, 2048, 128), BF16),
            jax.ShapeDtypeStruct((2, 128, 2048), BF16),
        ),
        in_specs=[vmem, any_space, any_space, any_space, any_space],
        out_specs=(vmem, vmem, any_space, any_space),
        scratch_shapes=[
            buf((256, 256), BF16), buf((256, 256), BF16),
            buf((2, 2048, 128), BF16), buf((2, 128, 2048), BF16),
            buf((2, 2048, 128), BF16), buf((2, 128, 2048), BF16),
            buf((8, 2, 256), F32),
            buf((16, 256), F32), buf((8, 16, 256), F32),
            buf((8, 8, 256), F32), buf((2, 4, 8, 256), F32),
            buf((8, 384), F32), buf((16, 8, 384), F32),
            buf((4, 8, 256), F32),
            buf((4, 8, 256), F32), buf((4, 8, 256), F32),
            buf((8, 256), F32), buf((16, 8, 256), F32),
            buf((2, 8, 256), F32), buf((8, 8, 256), F32),
            buf((32, 256), F32), buf((8, 32, 256), F32),
            buf((64, 1, 128), F32), buf((64, 1, 128), F32),
            buf((16, 256), F32), buf((16, 256), F32),
            pltpu.SemaphoreType.DMA((4,)), pltpu.SemaphoreType.DMA((2,)),
            pltpu.SemaphoreType.DMA((10,)), pltpu.SemaphoreType.DMA((10,)),
        ],
        compiler_params=pltpu.CompilerParams(
            collective_id=0, has_side_effects=True, vmem_limit_bytes=32 * 2**20
        ),
        name="soft_moe_backward",
    )(keys, tokens, cotangent, expert_in, expert_out)
    key_grad = key_row[0, :64].reshape(2, 32).T
    return (token_grad, key_grad, in_grad, out_grad)


def solution(mesh):
    return jax.shard_map(
        per_device,
        mesh=mesh,
        in_specs=(
            P("seq", "exp"),
            P("seq", "exp"),
            P(None, "exp"),
            P("exp", None, "seq"),
            P("exp", "seq", None),
        ),
        out_specs=(P("seq", "exp"), P("seq", "exp"), P("exp", None, "seq"), P("exp", "seq", None)),
        check_vma=False,
    )
```

```python
import jax
import jax.numpy as jnp
from jax import lax
from jax.experimental import pallas as pl
from jax.experimental.pallas import tpu as pltpu
from jax.sharding import PartitionSpec as P

MESH = pl.DeviceIdType.MESH
F32, BF16 = jnp.float32, jnp.bfloat16
ROOT_2_PI, CUBE = 0.7978845608, 0.044715


def dot(lhs, rhs, lhs_dim, rhs_dim):
    return lax.dot_general(
        lhs, rhs, (((lhs_dim,), (rhs_dim,)), ((), ())), preferred_element_type=F32
    )


def kernel(
    keys_hbm, tokens_hbm, cotan_hbm, win_hbm, wout_hbm,
    token_grad_ref, key_ref, in_grad, out_grad,
    key_raw, tok, cot, win, wout,
    key_src, key_buf, log_src, log_buf, c1_src, c1_buf, z_src, z_buf, d_buf,
    e1_src, e1_buf, e2_src, e2_buf, e3_src, e3_buf, g_src, g_buf, h_src, h_buf,
    gsi_rows, lse_rows, load_sem, meet_sem, send_sem, recv_sem,
):
    i, e = lax.axis_index("seq"), lax.axis_index("exp")
    x_lo, z, core = i // 32, (i // 2) % 16, i % 2
    pair, own = z // 2, 2 * (x_lo * 2 + core) + z % 2

    def seq_of(member, pair_at):
        return (member // 4) * 32 + (pair_at * 2 + member % 2) * 2 + (member // 2) % 2

    loads = [
        pltpu.make_async_copy(src, dst, load_sem.at[n])
        for n, (src, dst) in enumerate(
            ((keys_hbm, key_raw), (tokens_hbm, tok), (cotan_hbm, cot), (win_hbm, win), (wout_hbm, wout))
        )
    ]
    for load in loads:
        load.start()

    def signal(sem, seq_at, exp_at):
        pl.semaphore_signal(sem, 1, device_id=(seq_at, exp_at), device_id_type=MESH)

    def meet(step):
        signal(meet_sem.at[step], seq_of(own, (pair + 2**step) % 8), e)
        signal(meet_sem.at[step], seq_of(own, (pair + 8 - 2**step) % 8), e)

    def met(step):
        pl.semaphore_wait(meet_sem.at[step], 2)

    barrier = pltpu.get_barrier_semaphore()
    for k in range(1, 8):
        signal(barrier, i, (e + k) % 8)
    for k in range(1, 8):
        signal(barrier, seq_of((own + k) % 8, pair), e)
    for k in (1, 7):
        signal(barrier, seq_of(own, (pair + k) % 8), e)
    loads[0].wait()
    keys_wide = key_raw[...].astype(F32)
    for k in range(8):
        key_src[k] = keys_wide[:, 256 * k : 256 * k + 256]
    pl.semaphore_wait(barrier, 16)

    def send(phase, src, dst, seq_at, exp_at):
        pltpu.make_async_remote_copy(
            src, dst, send_sem.at[phase], recv_sem.at[phase],
            device_id=(seq_at, exp_at), device_id_type=MESH,
        ).start()

    def send_or_keep(phase, here, src, dst, seq_at, exp_at):
        @pl.when(here)
        def _():
            pltpu.make_async_copy(src, dst, recv_sem.at[phase]).start()

        @pl.when(jnp.logical_not(here))
        def _():
            send(phase, src, dst, seq_at, exp_at)

    def arrive(phase, ref):
        pltpu.make_async_copy(ref, ref, recv_sem.at[phase]).wait()

    def sent(phase, ref):
        pltpu.make_async_copy(ref, ref, send_sem.at[phase]).wait()

    def sent_some(phase, here, ref, count):
        @pl.when(here)
        def _():
            sent(phase, ref.at[pl.ds(0, count - 1)])

        @pl.when(jnp.logical_not(here))
        def _():
            sent(phase, ref)

    for k in range(1, 8):
        to = (e + k) % 8
        send(0, key_src.at[to], key_buf.at[e], i, to)
    meet(0)
    key_buf[e] = key_src[e]
    loads[1].wait()
    arrive(0, key_buf.at[pl.ds(0, 7)])
    keys = key_buf[...].reshape(16, 256).astype(BF16)

    log_src[...] = dot(keys, tok[...], 1, 1)
    for k in range(1, 8):
        to = (e + k) % 8
        send(1, log_src, log_buf.at[e], i, to)
    met(0)
    meet(1)
    log_buf[e] = log_src[...]
    loads[2].wait()
    arrive(1, log_buf.at[pl.ds(0, 7)])
    logits = log_buf[0]
    for k in range(1, 8):
        logits = logits + log_buf[k]

    peak = jnp.max(logits, axis=1, keepdims=True)
    weight_b = jnp.exp(logits - peak).astype(BF16)
    weight = weight_b.astype(F32)
    total = jnp.sum(weight, axis=1, keepdims=True)
    lse = peak + jnp.log(total)
    row_exp = jnp.exp(logits - jnp.max(logits, axis=0, keepdims=True))
    combine = row_exp / jnp.sum(row_exp, axis=0, keepdims=True)

    slot_part = dot(weight_b, tok[...], 1, 0) / total
    gout_part = dot(combine.astype(BF16), cot[...], 1, 0) * 8.0
    lse_wide = jnp.broadcast_to(lse, (16, 256))
    for b in range(8):
        c1_src[b, 0:2] = slot_part[2 * b : 2 * b + 2]
        c1_src[b, 2:4] = gout_part[2 * b : 2 * b + 2]
        c1_src[b, 4:6] = lse_wide[2 * b : 2 * b + 2]
        c1_src[b, 6:8] = jnp.zeros((2, 256), F32)
    home = seq_of(e, pair)
    c1_here = own == e
    send_or_keep(2, c1_here, c1_src.at[e], c1_buf.at[own], home, e)
    for k in range(1, 8):
        to = (e + k) % 8
        send(2, c1_src.at[to], c1_buf.at[own], home, to)
    met(1)
    arrive(2, c1_buf)
    part = [c1_buf[n] for n in range(8)]
    stat = [value[4:8] for value in part]
    top = stat[0]
    for n in range(1, 8):
        top = jnp.maximum(top, stat[n])
    norm, acc = jnp.zeros((4, 256), F32), jnp.zeros((4, 256), F32)
    for n in range(8):
        scale = jnp.exp(stat[n] - top)
        norm = norm + scale
        acc = acc + scale * part[n][0:4]
    row4 = lax.broadcasted_iota(jnp.int32, (4, 256), 0)
    first = row4 < 2
    z_src[:, 0:256] = jnp.where(first, acc / norm, acc)
    z_src[:, 256:384] = jnp.where(first, top + jnp.log(norm), 0.0)[:, 0:128]

    for k in range(1, 8):
        send(3, z_src, z_buf.at[pair], seq_of(own, (pair + k) % 8), e)
    z_buf[pair] = z_src[...]
    arrive(3, z_buf.at[pl.ds(0, 7)])
    top = z_buf[0, :, 256:384]
    for n in range(1, 8):
        top = jnp.maximum(top, z_buf[n, :, 256:384])
    norm = jnp.zeros((4, 128), F32)
    low, high = jnp.zeros((4, 128), F32), jnp.zeros((4, 128), F32)
    for n in range(8):
        scale = jnp.exp(z_buf[n, :, 256:384] - top)
        norm = norm + scale
        low = low + scale * z_buf[n, :, 0:128]
        high = high + scale * z_buf[n, :, 128:256]
    chunk = jnp.concatenate([low / norm, high / norm], axis=1)
    lse_all = top + jnp.log(norm)

    d_buf[own] = chunk
    for k in range(1, 8):
        send(4, d_buf.at[own], d_buf.at[own], seq_of((own + k) % 8, pair), e)
    loads[3].wait()
    loads[4].wait()
    arrive(4, d_buf.at[pl.ds(0, 7)])

    def win_at(n):
        at = n * 256
        return jnp.concatenate([win[0, at : at + 256, :], win[1, at : at + 256, :]], axis=1)

    def wout_at(n):
        return wout[:, :, n * 256 : n * 256 + 256].reshape(256, 256)

    vec = [d_buf[n].astype(BF16) for n in range(8)]
    pre = dot(vec[0], win_at(0), 1, 0)
    grad_hidden = dot(vec[0], wout_at(0), 1, 1)
    for n in range(1, 8):
        pre = pre + dot(vec[n], win_at(n), 1, 0)
        grad_hidden = grad_hidden + dot(vec[n], wout_at(n), 1, 1)
    pre, grad_hidden = pre[0:2], grad_hidden[2:4]
    tanh = jnp.tanh(ROOT_2_PI * (pre + CUBE * pre * pre * pre))
    hidden = 0.5 * pre * (1.0 + tanh)
    slope = 0.5 * (1.0 + tanh) + 0.5 * pre * (1.0 - tanh * tanh) * ROOT_2_PI * (
        1.0 + 3.0 * CUBE * pre * pre
    )
    lane4 = lax.broadcasted_iota(jnp.int32, (4, 256), 1)
    both = jnp.concatenate([grad_hidden * slope, hidden], axis=0)
    both = jnp.where((lane4 // 128) == (row4 % 2), both, 0.0)
    both_b = both.astype(BF16)

    for n in range(8):
        gin = dot(both_b, win_at(n), 1, 1)
        out = dot(both_b, wout_at(n), 1, 0)
        e1_src[n] = jnp.where(first, gin, out)
    for k in range(1, 8):
        to = (own + k) % 8
        send(5, e1_src.at[to], e1_buf.at[own], seq_of(to, pair), e)
    e1_buf[own] = e1_src[own]
    arrive(5, e1_buf.at[pl.ds(0, 7)])
    full = e1_buf[0]
    for n in range(1, 8):
        full = full + e1_buf[n]
    e2_src[...] = full
    for k in range(1, 8):
        send(6, e2_src, e2_buf.at[pair], seq_of(own, (pair + k) % 8), e)
    e2_buf[pair] = full

    pre_rows = jnp.where(first, both, 0.0).astype(BF16)
    hid_rows = jnp.where(first, 0.0, both).astype(BF16)
    for n in range(8):
        at = n * 256
        block = dot(vec[n], pre_rows, 0, 0).astype(BF16)
        in_grad[0, at : at + 256, :] = block[:, 0:128]
        in_grad[1, at : at + 256, :] = block[:, 128:256]
        block = dot(hid_rows, vec[n], 0, 0).astype(BF16)
        out_grad[:, :, at : at + 256] = block.reshape(2, 128, 256)

    arrive(6, e2_buf.at[pl.ds(0, 7)])
    full = e2_buf[0]
    for n in range(1, 8):
        full = full + e2_buf[n]
    full = full.astype(BF16).astype(F32)
    inner = jnp.sum(full * chunk, axis=1, keepdims=True)
    e3_src[0:4] = full
    e3_src[4:6] = jnp.concatenate([lse_all, lse_all], axis=1)[0:2]
    e3_src[6:8] = jnp.broadcast_to(inner, (4, 256))[0:2]

    send_or_keep(7, c1_here, e3_src, e3_buf.at[e], i, own)
    for k in range(1, 8):
        send(7, e3_src, e3_buf.at[e], seq_of((own + k) % 8, pair), own)
    arrive(7, e3_buf)
    stack = e3_buf[...].reshape(64, 256).astype(BF16)
    by_cot = dot(stack, cot[...], 1, 1)
    by_tok = dot(stack, tok[...], 1, 1)
    for b in range(8):
        g_src[2 * b : 2 * b + 2] = by_tok[8 * b : 8 * b + 2] - e3_buf[b, 6:8]
        g_src[16 + 2 * b : 18 + 2 * b] = by_cot[8 * b + 2 : 8 * b + 4]
    for k in range(1, 8):
        to = (e + k) % 8
        send(8, g_src, g_buf.at[e], i, to)
    g_buf[e] = g_src[...]
    for b in range(8):
        gsi_rows[2 * b : 2 * b + 2] = e3_buf[b, 0:2]
        lse_rows[2 * b : 2 * b + 2] = e3_buf[b, 4:6]
    dispatch = weight * (jnp.exp(lse - lse_rows[...]) / total)
    arrive(8, g_buf.at[pl.ds(0, 7)])
    grads = g_buf[0]
    for k in range(1, 8):
        grads = grads + g_buf[k]
    grad_dispatch, grad_combine = grads[0:16], grads[16:32]
    combine_row = jnp.sum(combine * grad_combine, axis=0, keepdims=True)
    grad_logits = dispatch * grad_dispatch + combine * (grad_combine - combine_row)
    grad_logits_b = grad_logits.astype(BF16)

    key_part = dot(grad_logits_b, tok[...], 1, 0)
    lane = lax.broadcasted_iota(jnp.int32, (16, 128), 1)
    for a in range(8):
        own = (key_part if a == 0 else pltpu.roll(key_part, 256 - 32 * a, 1))[:, 0:128]
        odd = pltpu.roll(pltpu.roll(own, 32, 1), 15, 0)
        row = jnp.where(lane < 32, own, odd)
        for b in range(8):
            h_src[a * 8 + b] = row[2 * b : 2 * b + 1]
    h_here = i // 8 == e
    for k in range(8):
        for m in range(8):
            a, b = (i + k) % 8, (e + m) % 8
            if k == 0 and m == 0:
                send_or_keep(9, h_here, h_src.at[a * 8 + b], h_buf.at[i], 8 * e + a, b)
            else:
                send(9, h_src.at[a * 8 + b], h_buf.at[i], 8 * e + a, b)

    left = jnp.concatenate([dispatch.astype(BF16), grad_logits_b], axis=0)
    right = jnp.concatenate([gsi_rows[...].astype(BF16), keys], axis=0)
    token_grad_ref[...] = dot(left, right, 0, 0).astype(BF16)
    arrive(9, h_buf)
    rows = h_buf[0]
    for n in range(1, 64):
        rows = rows + h_buf[n]
    key_ref[...] = jnp.concatenate([rows[:, 0:32], rows[:, 32:64]], axis=0)

    sent(0, key_buf.at[pl.ds(0, 7)])
    sent(1, log_buf.at[pl.ds(0, 7)])
    sent_some(2, c1_here, c1_src, 8)
    sent(3, z_buf.at[pl.ds(0, 7)])
    sent(4, d_buf.at[pl.ds(0, 7)])
    sent(5, e1_buf.at[pl.ds(0, 7)])
    sent(6, e2_buf.at[pl.ds(0, 7)])
    sent_some(7, c1_here, e3_buf, 8)
    sent(8, g_buf.at[pl.ds(0, 7)])
    sent_some(9, h_here, h_buf, 64)


def write_out(*refs):
    sems = refs[-1]
    count = (len(refs) - 1) // 2
    copies = [
        pltpu.make_async_copy(refs[n], refs[count + n], sems.at[n]) for n in range(count)
    ]
    for copy in copies:
        copy.start()
    for copy in copies:
        copy.wait()


def per_device(tokens, cotangent, slot_keys, expert_in, expert_out):
    any_space = pl.BlockSpec(memory_space=pl.ANY)
    buf = pltpu.VMEM
    outs = (
        ((256, 256), BF16), ((2, 32), F32), ((2, 2048, 128), BF16), ((2, 128, 2048), BF16)
    )
    big = [
        pltpu.with_memory_space_constraint(value, pltpu.HBM)
        for value in (slot_keys.T, tokens, cotangent, expert_in, expert_out)
    ]
    held = pl.pallas_call(
        kernel,
        out_shape=tuple(pltpu.VMEM(shape, kind) for shape, kind in outs),
        in_specs=[any_space] * 5,
        scratch_shapes=[
            buf((2, 2048), BF16), buf((256, 256), BF16), buf((256, 256), BF16),
            buf((2, 2048, 128), BF16), buf((2, 128, 2048), BF16),
            buf((8, 2, 256), F32), buf((8, 2, 256), F32),
            buf((16, 256), F32), buf((8, 16, 256), F32),
            buf((8, 8, 256), F32), buf((8, 8, 256), F32),
            buf((4, 384), F32), buf((8, 4, 384), F32),
            buf((8, 4, 256), F32),
            buf((8, 4, 256), F32), buf((8, 4, 256), F32),
            buf((4, 256), F32), buf((8, 4, 256), F32),
            buf((8, 256), F32), buf((8, 8, 256), F32),
            buf((32, 256), F32), buf((8, 32, 256), F32),
            buf((64, 1, 128), F32), buf((64, 1, 128), F32),
            buf((16, 256), F32), buf((16, 256), F32),
            pltpu.SemaphoreType.DMA((5,)),
            pltpu.SemaphoreType.REGULAR((2,)), pltpu.SemaphoreType.DMA((10,)), pltpu.SemaphoreType.DMA((10,)),
        ],
        compiler_params=pltpu.CompilerParams(
            collective_id=0, has_side_effects=True, vmem_limit_bytes=32 * 2**20
        ),
        name="soft_moe_backward",
    )(*big)
    token_grad, key_grad, in_grad, out_grad = pl.pallas_call(
        write_out,
        out_shape=tuple(pltpu.HBM(shape, kind) for shape, kind in outs),
        in_specs=[any_space] * 4,
        out_specs=(any_space,) * 4,
        scratch_shapes=[pltpu.SemaphoreType.DMA((4,))],
        compiler_params=pltpu.CompilerParams(vmem_limit_bytes=2**20),
        name="write_out",
    )(*held)
    return (token_grad, key_grad.T, in_grad, out_grad)


def solution(mesh):
    return jax.shard_map(
        per_device,
        mesh=mesh,
        in_specs=(
            P("seq", "exp"),
            P("seq", "exp"),
            P(None, "exp"),
            P("exp", None, "seq"),
            P("exp", "seq", None),
        ),
        out_specs=(P("seq", "exp"), P("seq", "exp"), P("exp", None, "seq"), P("exp", "seq", None)),
        check_vma=False,
    )
```

```python
import jax
import jax.numpy as jnp
from jax import lax
from jax.experimental import pallas as pl
from jax.experimental.pallas import tpu as pltpu
from jax.sharding import PartitionSpec as P

MESH = pl.DeviceIdType.MESH
F32, BF16 = jnp.float32, jnp.bfloat16
ROOT_2_PI, CUBE = 0.7978845608, 0.044715
EXP_FAR = ((1, 2), (1, 1), (1, 3), (1, 0), (0, 2), (0, 1), (0, 3))
PAIR_FAR = (4, 3, 5, 2, 6, 1, 7)
MEMBER_FAR = (7, 5, 6, 3, 4, 1, 2)


def dot(lhs, rhs, lhs_dim, rhs_dim):
    return lax.dot_general(
        lhs, rhs, (((lhs_dim,), (rhs_dim,)), ((), ())), preferred_element_type=F32
    )


def kernel(
    keys_hbm, tokens_hbm, cotan_hbm, win_hbm, wout_hbm,
    token_grad_ref, key_ref, in_grad, out_grad,
    key_raw, tok, cot, win, wout,
    key_src, key_buf, log_src, log_buf, c1_src, c1_buf, z_src, z_buf, d_buf,
    e1_src, e1_buf, e2_src, e2_buf, e3_src, e3_buf, g_src, g_buf, h_src, h_buf,
    win_by, win_to, wout_by, wout_to,
    load_sem, meet_sem, near_sem, send_sem, recv_sem,
):
    i, e = lax.axis_index("seq"), lax.axis_index("exp")
    x_lo, z, core = i // 32, (i // 2) % 16, i % 2
    pair, own = z // 2, 2 * (x_lo * 2 + core) + z % 2

    def seq_of(member, pair_at):
        return (member // 4) * 32 + (pair_at * 2 + member % 2) * 2 + (member // 2) % 2

    loads = [
        pltpu.make_async_copy(src, dst, load_sem.at[n])
        for n, (src, dst) in enumerate(
            ((keys_hbm, key_raw), (tokens_hbm, tok), (cotan_hbm, cot), (win_hbm, win), (wout_hbm, wout))
        )
    ]
    for load in loads:
        load.start()

    def exp_at(step):
        return (e // 4 + step[0]) % 2 * 4 + (e + step[1]) % 4

    def member(step):
        return (
            (own // 4 + step // 4) % 2 * 4 + (own // 2 + step // 2) % 2 * 2 + (own + step) % 2
        )

    def signal(sem, seq_at, exp_at):
        pl.semaphore_signal(sem, 1, device_id=(seq_at, exp_at), device_id_type=MESH)

    def meet(step):
        signal(meet_sem.at[step], seq_of(own, (pair + 2**step) % 8), e)
        signal(meet_sem.at[step], seq_of(own, (pair + 8 - 2**step) % 8), e)

    def met(step):
        pl.semaphore_wait(meet_sem.at[step], 2)

    barrier = pltpu.get_barrier_semaphore()
    for step in EXP_FAR:
        signal(barrier, i, exp_at(step))
    for step in MEMBER_FAR:
        signal(barrier, seq_of(member(step), pair), e)
    for k in (1, 7):
        signal(barrier, seq_of(own, (pair + k) % 8), e)
    loads[0].wait()
    keys_wide = key_raw[...].astype(F32)
    for k in range(8):
        key_src[k] = keys_wide[:, 256 * k : 256 * k + 256]
    pl.semaphore_wait(barrier, 16)

    def send(phase, src, dst, seq_at, exp_at):
        pltpu.make_async_remote_copy(
            src, dst, send_sem.at[phase], recv_sem.at[phase],
            device_id=(seq_at, exp_at), device_id_type=MESH,
        ).start()

    def send_or_keep(phase, here, src, dst, seq_at, exp_at):
        @pl.when(here)
        def _():
            pltpu.make_async_copy(src, dst, recv_sem.at[phase]).start()

        @pl.when(jnp.logical_not(here))
        def _():
            send(phase, src, dst, seq_at, exp_at)

    def arrive(phase, ref):
        pltpu.make_async_copy(ref, ref, recv_sem.at[phase]).wait()

    def sent(phase, ref):
        pltpu.make_async_copy(ref, ref, send_sem.at[phase]).wait()

    def sent_some(phase, here, ref, count):
        @pl.when(here)
        def _():
            sent(phase, ref.at[pl.ds(0, count - 1)])

        @pl.when(jnp.logical_not(here))
        def _():
            sent(phase, ref)

    for step in EXP_FAR:
        to = exp_at(step)
        send(0, key_src.at[to], key_buf.at[e], i, to)
    meet(0)
    key_buf[e] = key_src[e]
    loads[1].wait()
    arrive(0, key_buf.at[pl.ds(0, 7)])
    keys = key_buf[...].reshape(16, 256).astype(BF16)

    log_src[...] = dot(keys, tok[...], 1, 1)
    for step in EXP_FAR:
        to = exp_at(step)
        send(1, log_src, log_buf.at[e], i, to)
    met(0)
    meet(1)
    log_buf[e] = log_src[...]
    loads[2].wait()
    arrive(1, log_buf.at[pl.ds(0, 7)])
    logits = log_buf[0]
    for k in range(1, 8):
        logits = logits + log_buf[k]

    peak = jnp.max(logits, axis=1, keepdims=True)
    weight_b = jnp.exp(logits - peak).astype(BF16)
    weight = weight_b.astype(F32)
    total = jnp.sum(weight, axis=1, keepdims=True)
    lse = peak + jnp.log(total)
    row_exp = jnp.exp(logits - jnp.max(logits, axis=0, keepdims=True))
    combine = row_exp / jnp.sum(row_exp, axis=0, keepdims=True)

    slot_part = dot(weight_b, tok[...], 1, 0) / total
    gout_part = dot(combine.astype(BF16), cot[...], 1, 0) * 8.0
    lse_wide = jnp.broadcast_to(lse, (16, 128))
    for b in range(8):
        c1_src[b, 0:2, 0:256] = slot_part[2 * b : 2 * b + 2]
        c1_src[b, 2:4, 0:256] = gout_part[2 * b : 2 * b + 2]
        c1_src[b, 0:2, 256:384] = lse_wide[2 * b : 2 * b + 2]
        c1_src[b, 2:4, 256:384] = jnp.zeros((2, 128), F32)
    home = seq_of(e, pair)
    c1_here = own == e
    for step in EXP_FAR:
        to = exp_at(step)
        send(2, c1_src.at[to], c1_buf.at[own], home, to)
    send_or_keep(2, c1_here, c1_src.at[e], c1_buf.at[own], home, e)
    share = weight / total
    met(1)
    arrive(2, c1_buf)
    def merged(buf):
        top = buf[0, :, 256:384]
        for n in range(1, 8):
            top = jnp.maximum(top, buf[n, :, 256:384])
        norm = jnp.zeros((4, 128), F32)
        low, high = jnp.zeros((4, 128), F32), jnp.zeros((4, 128), F32)
        for n in range(8):
            scale = jnp.exp(buf[n, :, 256:384] - top)
            norm = norm + scale
            low = low + scale * buf[n, :, 0:128]
            high = high + scale * buf[n, :, 128:256]
        return low, high, norm, top + jnp.log(norm)

    row4 = lax.broadcasted_iota(jnp.int32, (4, 256), 0)
    first = row4 < 2
    first_tile = first[:, 0:128]
    low, high, norm, lse_all = merged(c1_buf)
    norm = jnp.where(first_tile, norm, 1.0)
    z_src[:, 0:128] = low / norm
    z_src[:, 128:256] = high / norm
    z_src[:, 256:384] = jnp.where(first_tile, lse_all, 0.0)

    for k in PAIR_FAR:
        send(3, z_src, z_buf.at[pair], seq_of(own, (pair + k) % 8), e)
    z_buf[pair] = z_src[...]
    loads[3].wait()
    loads[4].wait()
    for n in range(8):
        at = n * 256
        pair_in = jnp.concatenate([win[0, at : at + 256, :], win[1, at : at + 256, :]], axis=1)
        win_by[n] = pair_in
        win_to[n] = pair_in.T
        pair_out = wout[:, :, at : at + 256].reshape(256, 256)
        wout_to[n] = pair_out
        wout_by[n] = pair_out.T
    arrive(3, z_buf.at[pl.ds(0, 7)])
    low, high, norm, lse_all = merged(z_buf)
    chunk = jnp.concatenate([low / norm, high / norm], axis=1)

    d_buf[own] = chunk
    for step in MEMBER_FAR:
        pltpu.make_async_remote_copy(
            d_buf.at[own], d_buf.at[own], send_sem.at[4], near_sem.at[step],
            device_id=(seq_of(member(step), pair), e), device_id_type=MESH,
        ).start()
    vec = chunk.astype(BF16)
    pre = dot(vec, win_by[own], 1, 0)
    grad_hidden = dot(vec, wout_by[own], 1, 0)
    for step in MEMBER_FAR[::-1]:
        n = member(step)
        pltpu.make_async_copy(d_buf.at[n], d_buf.at[n], near_sem.at[step]).wait()
        vec = d_buf[n].astype(BF16)
        pre = pre + dot(vec, win_by[n], 1, 0)
        grad_hidden = grad_hidden + dot(vec, wout_by[n], 1, 0)
    pre, grad_hidden = pre[0:2], grad_hidden[2:4]
    tanh = jnp.tanh(ROOT_2_PI * (pre + CUBE * pre * pre * pre))
    hidden = 0.5 * pre * (1.0 + tanh)
    slope = 0.5 * (1.0 + tanh) + 0.5 * pre * (1.0 - tanh * tanh) * ROOT_2_PI * (
        1.0 + 3.0 * CUBE * pre * pre
    )
    lane4 = lax.broadcasted_iota(jnp.int32, (4, 256), 1)
    both = jnp.concatenate([grad_hidden * slope, hidden], axis=0)
    both = jnp.where((lane4 // 128) == (row4 % 2), both, 0.0)
    both_b = both.astype(BF16)

    def partial(n):
        return jnp.where(first, dot(both_b, win_to[n], 1, 0), dot(both_b, wout_to[n], 1, 0))

    for step in MEMBER_FAR:
        to = member(step)
        e1_src[step] = partial(to)
        send(5, e1_src.at[step], e1_buf.at[step], seq_of(to, pair), e)
    full = partial(own)
    arrive(5, e1_buf.at[pl.ds(1, 7)])
    for n in range(1, 8):
        full = full + e1_buf[n]
    e2_src[...] = full
    for k in PAIR_FAR:
        send(6, e2_src, e2_buf.at[pair], seq_of(own, (pair + k) % 8), e)
    e2_buf[pair] = full

    pre_rows = jnp.where(first, both, 0.0).astype(BF16)
    hid_rows = jnp.where(first, 0.0, both).astype(BF16)
    for n in range(8):
        at = n * 256
        vec = d_buf[n].astype(BF16)
        block = dot(vec, pre_rows, 0, 0).astype(BF16)
        in_grad[0, at : at + 256, :] = block[:, 0:128]
        in_grad[1, at : at + 256, :] = block[:, 128:256]
        block = dot(hid_rows, vec, 0, 0).astype(BF16)
        out_grad[:, :, at : at + 256] = block.reshape(2, 128, 256)

    arrive(6, e2_buf.at[pl.ds(0, 7)])
    full = e2_buf[0]
    for n in range(1, 8):
        full = full + e2_buf[n]
    full = full.astype(BF16).astype(F32)
    inner = jnp.sum(full * chunk, axis=1, keepdims=True)
    e3_src[0] = full[0:2]
    e3_src[1] = full[2:4]
    e3_src[2] = jnp.concatenate([lse_all, lse_all], axis=1)[0:2]
    e3_src[3] = jnp.broadcast_to(inner, (4, 256))[0:2]

    for step in MEMBER_FAR:
        send(7, e3_src, e3_buf.at[e], seq_of(member(step), pair), own)
    send_or_keep(7, c1_here, e3_src, e3_buf.at[e], i, own)
    arrive(7, e3_buf)

    def rows_of(kind):
        return e3_buf[:, kind].reshape(16, 256)

    gsi_b = rows_of(0).astype(BF16)
    grad_combine = dot(rows_of(1).astype(BF16), cot[...], 1, 1)
    grad_dispatch = dot(gsi_b, tok[...], 1, 1) - rows_of(3)
    dispatch = share * jnp.exp(lse - rows_of(2))
    combine_row = jnp.sum(combine * grad_combine, axis=0, keepdims=True)
    grad_part = dispatch * grad_dispatch + combine * (grad_combine - combine_row)
    g_src[...] = grad_part
    for step in EXP_FAR:
        send(8, g_src, g_buf.at[e], i, exp_at(step))
    g_buf[e] = grad_part
    arrive(8, g_buf.at[pl.ds(0, 7)])
    grads = g_buf[0]
    for k in range(1, 8):
        grads = grads + g_buf[k]
    grad_logits_b = grads.astype(BF16)

    key_part = dot(grad_logits_b, tok[...], 1, 0)
    lane = lax.broadcasted_iota(jnp.int32, (16, 128), 1)
    for a in range(8):
        own = (key_part if a == 0 else pltpu.roll(key_part, 256 - 32 * a, 1))[:, 0:128]
        odd = pltpu.roll(pltpu.roll(own, 32, 1), 15, 0)
        row = jnp.where(lane < 32, own, odd)
        for b in range(8):
            h_src[a * 8 + b] = row[2 * b : 2 * b + 1]
    h_here = i // 8 == e
    for step in EXP_FAR + ((0, 0),):
        b = exp_at(step)
        for k in list(range(1, 8)) + [0]:
            a = (i + k) % 8
            if k == 0 and step == (0, 0):
                send_or_keep(9, h_here, h_src.at[a * 8 + b], h_buf.at[i], 8 * e + a, b)
            else:
                send(9, h_src.at[a * 8 + b], h_buf.at[i], 8 * e + a, b)

    left = jnp.concatenate([dispatch.astype(BF16), grad_logits_b], axis=0)
    right = jnp.concatenate([gsi_b, keys], axis=0)
    token_grad_ref[...] = dot(left, right, 0, 0).astype(BF16)
    arrive(9, h_buf)
    rows = h_buf[0]
    for n in range(1, 64):
        rows = rows + h_buf[n]
    key_ref[...] = jnp.concatenate([rows[:, 0:32], rows[:, 32:64]], axis=0)

    sent(0, key_buf.at[pl.ds(0, 7)])
    sent(1, log_buf.at[pl.ds(0, 7)])
    sent_some(2, c1_here, c1_src, 8)
    sent(3, z_buf.at[pl.ds(0, 7)])
    sent(4, d_buf.at[pl.ds(0, 7)])
    sent(5, e1_buf.at[pl.ds(0, 7)])
    sent(6, e2_buf.at[pl.ds(0, 7)])
    sent_some(7, c1_here, e3_buf, 8)
    sent(8, g_buf.at[pl.ds(0, 7)])
    sent_some(9, h_here, h_buf, 64)


def write_out(*refs):
    sems = refs[-1]
    pieces = []
    for src, dst in zip(refs[2:4], refs[6:8]):
        rows = src.shape[1] // 4
        for n in range(2):
            for m in range(4):
                part = pl.ds(m * rows, rows)
                pieces.append((src.at[n, part], dst.at[n, part]))
    pieces += list(zip(refs[0:2], refs[4:6]))
    copies = [pltpu.make_async_copy(src, dst, sems.at[n]) for n, (src, dst) in enumerate(pieces)]
    for copy in copies:
        copy.start()
    for copy in copies:
        copy.wait()


def per_device(tokens, cotangent, slot_keys, expert_in, expert_out):
    any_space = pl.BlockSpec(memory_space=pl.ANY)
    buf = pltpu.VMEM
    outs = (
        ((256, 256), BF16), ((2, 32), F32), ((2, 2048, 128), BF16), ((2, 128, 2048), BF16)
    )
    big = [
        pltpu.with_memory_space_constraint(value, pltpu.HBM)
        for value in (slot_keys.T, tokens, cotangent, expert_in, expert_out)
    ]
    held = pl.pallas_call(
        kernel,
        out_shape=tuple(pltpu.VMEM(shape, kind) for shape, kind in outs),
        in_specs=[any_space] * 5,
        scratch_shapes=[
            buf((2, 2048), BF16), buf((256, 256), BF16), buf((256, 256), BF16),
            buf((2, 2048, 128), BF16), buf((2, 128, 2048), BF16),
            buf((8, 2, 256), F32), buf((8, 2, 256), F32),
            buf((16, 256), F32), buf((8, 16, 256), F32),
            buf((8, 4, 384), F32), buf((8, 4, 384), F32),
            buf((4, 384), F32), buf((8, 4, 384), F32),
            buf((8, 4, 256), F32),
            buf((8, 4, 256), F32), buf((8, 4, 256), F32),
            buf((4, 256), F32), buf((8, 4, 256), F32),
            buf((4, 2, 256), F32), buf((8, 4, 2, 256), F32),
            buf((16, 256), F32), buf((8, 16, 256), F32),
            buf((64, 1, 128), F32), buf((64, 1, 128), F32),
            buf((8, 256, 256), BF16), buf((8, 256, 256), BF16),
            buf((8, 256, 256), BF16), buf((8, 256, 256), BF16),
            pltpu.SemaphoreType.DMA((5,)),
            pltpu.SemaphoreType.REGULAR((2,)), pltpu.SemaphoreType.DMA((8,)),
            pltpu.SemaphoreType.DMA((10,)), pltpu.SemaphoreType.DMA((10,)),
        ],
        compiler_params=pltpu.CompilerParams(
            collective_id=0, has_side_effects=True, vmem_limit_bytes=32 * 2**20
        ),
        name="soft_moe_backward",
    )(*big)
    token_grad, key_grad, in_grad, out_grad = pl.pallas_call(
        write_out,
        out_shape=tuple(pltpu.HBM(shape, kind) for shape, kind in outs),
        in_specs=[any_space] * 4,
        out_specs=(any_space,) * 4,
        scratch_shapes=[pltpu.SemaphoreType.DMA((18,))],
        compiler_params=pltpu.CompilerParams(vmem_limit_bytes=2**20),
        name="write_out",
    )(*held)
    return (token_grad, key_grad.T, in_grad, out_grad)


def solution(mesh):
    return jax.shard_map(
        per_device,
        mesh=mesh,
        in_specs=(
            P("seq", "exp"),
            P("seq", "exp"),
            P(None, "exp"),
            P("exp", None, "seq"),
            P("exp", "seq", None),
        ),
        out_specs=(P("seq", "exp"), P("seq", "exp"), P("exp", None, "seq"), P("exp", "seq", None)),
        check_vma=False,
    )
```

```python
import jax
import jax.numpy as jnp
from jax import lax
from jax.experimental import pallas as pl
from jax.experimental.pallas import tpu as pltpu
from jax.sharding import PartitionSpec as P

MESH = pl.DeviceIdType.MESH
F32, BF16 = jnp.float32, jnp.bfloat16
ROOT_2_PI, CUBE = 0.7978845608, 0.044715
EXP_FAR = ((1, 2), (1, 1), (1, 3), (1, 0), (0, 2), (0, 1), (0, 3))
PAIR_FAR = (4, 3, 5, 2, 6, 1, 7)
MEMBER_FAR = (7, 5, 6, 3, 4, 1, 2)


def dot(lhs, rhs, lhs_dim, rhs_dim):
    return lax.dot_general(
        lhs, rhs, (((lhs_dim,), (rhs_dim,)), ((), ())), preferred_element_type=F32
    )


def kernel(
    keys_hbm, tokens_hbm, cotan_hbm, win_hbm, wout_hbm,
    token_grad_ref, key_ref, in_grad, out_grad,
    key_raw, tok, cot, win, wout,
    key_src, key_buf, log_src, log_buf, c1_src, c1_buf, z_src, z_buf, d_buf,
    e1_src, e1_buf, e2_src, e2_buf, e3_src, e3_buf, g_src, g_buf, h_src, h_buf,
    lse_src, lse_buf, tok_t, cot_t,
    win_by, win_to, wout_by, wout_to,
    load_sem, meet_sem, near_sem, send_sem, recv_sem,
):
    i, e = lax.axis_index("seq"), lax.axis_index("exp")
    x_lo, z, core = i // 32, (i // 2) % 16, i % 2
    pair, own = z // 2, 2 * (x_lo * 2 + core) + z % 2

    def seq_of(member, pair_at):
        return (member // 4) * 32 + (pair_at * 2 + member % 2) * 2 + (member // 2) % 2

    loads = [
        pltpu.make_async_copy(src, dst, load_sem.at[n])
        for n, (src, dst) in enumerate(
            ((keys_hbm, key_raw), (tokens_hbm, tok), (cotan_hbm, cot), (win_hbm, win), (wout_hbm, wout))
        )
    ]
    for load in loads:
        load.start()

    def exp_at(step):
        return (e // 4 + step[0]) % 2 * 4 + (e + step[1]) % 4

    def member(step):
        return (
            (own // 4 + step // 4) % 2 * 4 + (own // 2 + step // 2) % 2 * 2 + (own + step) % 2
        )

    def signal(sem, seq_at, exp_at):
        pl.semaphore_signal(sem, 1, device_id=(seq_at, exp_at), device_id_type=MESH)

    def meet(step):
        signal(meet_sem.at[step], seq_of(own, (pair + 2**step) % 8), e)
        signal(meet_sem.at[step], seq_of(own, (pair + 8 - 2**step) % 8), e)

    def met(step):
        pl.semaphore_wait(meet_sem.at[step], 2)

    barrier = pltpu.get_barrier_semaphore()
    for step in EXP_FAR:
        signal(barrier, i, exp_at(step))
    for step in MEMBER_FAR:
        signal(barrier, seq_of(member(step), pair), e)
    for k in (1, 7):
        signal(barrier, seq_of(own, (pair + k) % 8), e)
    loads[0].wait()
    keys_wide = key_raw[...].astype(F32)
    for k in range(8):
        key_src[k] = keys_wide[:, 256 * k : 256 * k + 256]
    loads[1].wait()
    tok_t[...] = tok[...].T
    pl.semaphore_wait(barrier, 16)

    def send(phase, src, dst, seq_at, exp_at):
        pltpu.make_async_remote_copy(
            src, dst, send_sem.at[phase], recv_sem.at[phase],
            device_id=(seq_at, exp_at), device_id_type=MESH,
        ).start()

    def send_or_keep(phase, here, src, dst, seq_at, exp_at):
        @pl.when(here)
        def _():
            pltpu.make_async_copy(src, dst, recv_sem.at[phase]).start()

        @pl.when(jnp.logical_not(here))
        def _():
            send(phase, src, dst, seq_at, exp_at)

    def arrive(phase, ref):
        pltpu.make_async_copy(ref, ref, recv_sem.at[phase]).wait()

    def send_near(step, src, dst, seq_at, exp_at):
        pltpu.make_async_remote_copy(
            src, dst, send_sem.at[4], near_sem.at[step],
            device_id=(seq_at, exp_at), device_id_type=MESH,
        ).start()

    def arrive_near(step, ref):
        pltpu.make_async_copy(ref, ref, near_sem.at[step]).wait()

    def sent(phase, ref):
        pltpu.make_async_copy(ref, ref, send_sem.at[phase]).wait()

    def sent_some(phase, here, ref, count):
        @pl.when(here)
        def _():
            sent(phase, ref.at[pl.ds(0, count - 1)])

        @pl.when(jnp.logical_not(here))
        def _():
            sent(phase, ref)

    for step in EXP_FAR:
        to = exp_at(step)
        send(0, key_src.at[to], key_buf.at[e], i, to)
    meet(0)
    key_buf[e] = key_src[e]
    arrive(0, key_buf.at[pl.ds(0, 7)])
    keys = key_buf[...].reshape(16, 256).astype(BF16)

    log_src[...] = dot(keys, tok_t[...], 1, 0)
    for step in EXP_FAR:
        to = exp_at(step)
        send(1, log_src, log_buf.at[e], i, to)
    met(0)
    meet(1)
    log_buf[e] = log_src[...]
    loads[2].wait()
    arrive(1, log_buf.at[pl.ds(0, 7)])
    logits = log_buf[0]
    for k in range(1, 8):
        logits = logits + log_buf[k]

    peak = jnp.max(logits, axis=1, keepdims=True)
    weight_b = jnp.exp(logits - peak).astype(BF16)
    weight = weight_b.astype(F32)
    total = jnp.sum(weight, axis=1, keepdims=True)
    lse = peak + jnp.log(total)
    row_exp = jnp.exp(logits - jnp.max(logits, axis=0, keepdims=True))
    combine = row_exp / jnp.sum(row_exp, axis=0, keepdims=True)

    slot_part = dot(weight_b, tok[...], 1, 0) / total
    gout_part = dot(combine.astype(BF16), cot[...], 1, 0) * 8.0
    lse_wide = jnp.broadcast_to(lse, (16, 128))
    for b in range(8):
        c1_src[b, 0:2, 0:256] = slot_part[2 * b : 2 * b + 2]
        c1_src[b, 2:4, 0:256] = gout_part[2 * b : 2 * b + 2]
        c1_src[b, 0:2, 256:384] = lse_wide[2 * b : 2 * b + 2]
        c1_src[b, 2:4, 256:384] = jnp.zeros((2, 128), F32)
    home = seq_of(e, pair)
    c1_here = own == e
    for step in EXP_FAR:
        to = exp_at(step)
        send(2, c1_src.at[to], c1_buf.at[own], home, to)
    send_or_keep(2, c1_here, c1_src.at[e], c1_buf.at[own], home, e)
    share = weight / total
    met(1)
    arrive(2, c1_buf)
    def merged(buf):
        top = buf[0, :, 256:384]
        for n in range(1, 8):
            top = jnp.maximum(top, buf[n, :, 256:384])
        norm = jnp.zeros((4, 128), F32)
        low, high = jnp.zeros((4, 128), F32), jnp.zeros((4, 128), F32)
        for n in range(8):
            scale = jnp.exp(buf[n, :, 256:384] - top)
            norm = norm + scale
            low = low + scale * buf[n, :, 0:128]
            high = high + scale * buf[n, :, 128:256]
        return low, high, norm, top + jnp.log(norm)

    row4 = lax.broadcasted_iota(jnp.int32, (4, 256), 0)
    first = row4 < 2
    first_tile = first[:, 0:128]
    low, high, norm, lse_all = merged(c1_buf)
    norm = jnp.where(first_tile, norm, 1.0)
    z_src[:, 0:128] = low / norm
    z_src[:, 128:256] = high / norm
    z_src[:, 256:384] = jnp.where(first_tile, lse_all, 0.0)

    for k in PAIR_FAR:
        send(3, z_src, z_buf.at[pair], seq_of(own, (pair + k) % 8), e)
    z_buf[pair] = z_src[...]
    loads[3].wait()
    loads[4].wait()
    for n in range(8):
        at = n * 256
        pair_in = jnp.concatenate([win[0, at : at + 256, :], win[1, at : at + 256, :]], axis=1)
        win_by[n] = pair_in
        win_to[n] = pair_in.T
        pair_out = wout[:, :, at : at + 256].reshape(256, 256)
        wout_to[n] = pair_out
        wout_by[n] = pair_out.T
    cot_t[...] = cot[...].T
    arrive(3, z_buf.at[pl.ds(0, 7)])
    low, high, norm, lse_all = merged(z_buf)
    chunk = jnp.concatenate([low / norm, high / norm], axis=1)

    d_buf[own] = chunk
    for step in MEMBER_FAR:
        send_near(step, d_buf.at[own], d_buf.at[own], seq_of(member(step), pair), e)
    vec = chunk.astype(BF16)
    pre = dot(vec, win_by[own], 1, 0)
    grad_hidden = dot(vec, wout_by[own], 1, 0)
    for step in MEMBER_FAR[::-1]:
        n = member(step)
        arrive_near(step, d_buf.at[n])
        vec = d_buf[n].astype(BF16)
        pre = pre + dot(vec, win_by[n], 1, 0)
        grad_hidden = grad_hidden + dot(vec, wout_by[n], 1, 0)
    pre, grad_hidden = pre[0:2], grad_hidden[2:4]
    tanh = jnp.tanh(ROOT_2_PI * (pre + CUBE * pre * pre * pre))
    hidden = 0.5 * pre * (1.0 + tanh)
    slope = 0.5 * (1.0 + tanh) + 0.5 * pre * (1.0 - tanh * tanh) * ROOT_2_PI * (
        1.0 + 3.0 * CUBE * pre * pre
    )
    lane4 = lax.broadcasted_iota(jnp.int32, (4, 256), 1)
    both = jnp.concatenate([grad_hidden * slope, hidden], axis=0)
    both = jnp.where((lane4 // 128) == (row4 % 2), both, 0.0)
    both_b = both.astype(BF16)

    def partial(n):
        return jnp.where(first, dot(both_b, win_to[n], 1, 0), dot(both_b, wout_to[n], 1, 0))

    for step in MEMBER_FAR:
        to = member(step)
        e1_src[step] = partial(to)
        send(5, e1_src.at[step], e1_buf.at[step], seq_of(to, pair), e)
    full = partial(own)
    arrive(5, e1_buf.at[pl.ds(1, 7)])
    for n in range(1, 8):
        full = full + e1_buf[n]
    e2_src[...] = full
    for k in PAIR_FAR:
        send(6, e2_src, e2_buf.at[pair], seq_of(own, (pair + k) % 8), e)
    e2_buf[pair] = full

    lse_src[...] = lse_all[0:2]
    for step in EXP_FAR:
        send(10, lse_src, lse_buf.at[e], i, exp_at(step))
    lse_buf[e] = lse_all[0:2]
    pre_rows = jnp.where(first, both, 0.0).astype(BF16)
    hid_rows = jnp.where(first, 0.0, both).astype(BF16)
    for n in range(8):
        at = n * 256
        vec = d_buf[n].astype(BF16)
        block = dot(vec, pre_rows, 0, 0).astype(BF16)
        in_grad[0, at : at + 256, :] = block[:, 0:128]
        in_grad[1, at : at + 256, :] = block[:, 128:256]
        block = dot(hid_rows, vec, 0, 0).astype(BF16)
        out_grad[:, :, at : at + 256] = block.reshape(2, 128, 256)

    arrive(10, lse_buf.at[pl.ds(0, 7)])
    lse_rows = lse_buf[...].reshape(16, 128)
    dispatch = share * jnp.exp(lse - jnp.concatenate([lse_rows, lse_rows], axis=1))
    arrive(6, e2_buf.at[pl.ds(0, 7)])
    full = e2_buf[0]
    for n in range(1, 8):
        full = full + e2_buf[n]
    full = full.astype(BF16).astype(F32)
    inner = jnp.sum(full * chunk, axis=1, keepdims=True)
    e3_src[0] = full[0:2]
    e3_src[1] = full[2:4]
    e3_src[2] = jnp.broadcast_to(inner, (4, 256))[0:2]

    for step in MEMBER_FAR:
        send(7, e3_src, e3_buf.at[e], seq_of(member(step), pair), own)
    send_or_keep(7, c1_here, e3_src, e3_buf.at[e], i, own)
    arrive(7, e3_buf)

    def rows_of(kind):
        return e3_buf[:, kind].reshape(16, 256)

    gsi_b = rows_of(0).astype(BF16)
    grad_combine = dot(rows_of(1).astype(BF16), cot_t[...], 1, 0)
    grad_dispatch = dot(gsi_b, tok_t[...], 1, 0) - rows_of(2)
    combine_row = jnp.sum(combine * grad_combine, axis=0, keepdims=True)
    grad_part = dispatch * grad_dispatch + combine * (grad_combine - combine_row)
    grad_part = grad_part.astype(BF16)
    g_src[...] = grad_part
    for step in EXP_FAR:
        send(8, g_src, g_buf.at[e], i, exp_at(step))
    g_buf[e] = grad_part
    arrive(8, g_buf.at[pl.ds(0, 7)])
    grads = g_buf[0].astype(F32)
    for k in range(1, 8):
        grads = grads + g_buf[k].astype(F32)
    grad_logits_b = grads.astype(BF16)

    key_part = dot(grad_logits_b, tok[...], 1, 0)
    lane = lax.broadcasted_iota(jnp.int32, (16, 128), 1)
    for a in range(8):
        own = (key_part if a == 0 else pltpu.roll(key_part, 256 - 32 * a, 1))[:, 0:128]
        odd = pltpu.roll(pltpu.roll(own, 32, 1), 15, 0)
        row = jnp.where(lane < 32, own, odd)
        for b in range(8):
            h_src[a * 8 + b] = row[2 * b : 2 * b + 1]
    h_here = i // 8 == e
    for step in EXP_FAR + ((0, 0),):
        b = exp_at(step)
        for k in list(range(1, 8)) + [0]:
            a = (i + k) % 8
            if k == 0 and step == (0, 0):
                send_or_keep(9, h_here, h_src.at[a * 8 + b], h_buf.at[i], 8 * e + a, b)
            else:
                send(9, h_src.at[a * 8 + b], h_buf.at[i], 8 * e + a, b)

    left = jnp.concatenate([dispatch.astype(BF16), grad_logits_b], axis=0)
    right = jnp.concatenate([gsi_b, keys], axis=0)
    token_grad_ref[...] = dot(left, right, 0, 0).astype(BF16)
    arrive(9, h_buf)
    rows = h_buf[0]
    for n in range(1, 64):
        rows = rows + h_buf[n]
    key_ref[...] = jnp.concatenate([rows[:, 0:32], rows[:, 32:64]], axis=0)

    sent(0, key_buf.at[pl.ds(0, 7)])
    sent(1, log_buf.at[pl.ds(0, 7)])
    sent_some(2, c1_here, c1_src, 8)
    sent(3, z_buf.at[pl.ds(0, 7)])
    sent(4, d_buf.at[pl.ds(0, 7)])
    sent(5, e1_buf.at[pl.ds(0, 7)])
    sent(6, e2_buf.at[pl.ds(0, 7)])
    sent_some(7, c1_here, e3_buf, 8)
    sent(8, g_buf.at[pl.ds(0, 7)])
    sent_some(9, h_here, h_buf, 64)
    sent(10, lse_buf.at[pl.ds(0, 7)])


def write_out(*refs):
    sems = refs[-1]
    count = (len(refs) - 1) // 2
    copies = [
        pltpu.make_async_copy(refs[n], refs[count + n], sems.at[n]) for n in range(count)
    ]
    for copy in copies:
        copy.start()
    for copy in copies:
        copy.wait()


def per_device(tokens, cotangent, slot_keys, expert_in, expert_out):
    any_space = pl.BlockSpec(memory_space=pl.ANY)
    buf = pltpu.VMEM
    outs = (
        ((256, 256), BF16), ((2, 32), F32), ((2, 2048, 128), BF16), ((2, 128, 2048), BF16)
    )
    big = [
        pltpu.with_memory_space_constraint(value, pltpu.HBM)
        for value in (slot_keys.T, tokens, cotangent, expert_in, expert_out)
    ]
    held = pl.pallas_call(
        kernel,
        out_shape=tuple(pltpu.VMEM(shape, kind) for shape, kind in outs),
        in_specs=[any_space] * 5,
        scratch_shapes=[
            buf((2, 2048), BF16), buf((256, 256), BF16), buf((256, 256), BF16),
            buf((2, 2048, 128), BF16), buf((2, 128, 2048), BF16),
            buf((8, 2, 256), F32), buf((8, 2, 256), F32),
            buf((16, 256), F32), buf((8, 16, 256), F32),
            buf((8, 4, 384), F32), buf((8, 4, 384), F32),
            buf((4, 384), F32), buf((8, 4, 384), F32),
            buf((8, 4, 256), F32),
            buf((8, 4, 256), F32), buf((8, 4, 256), F32),
            buf((4, 256), F32), buf((8, 4, 256), F32),
            buf((3, 2, 256), F32), buf((8, 3, 2, 256), F32),
            buf((16, 256), BF16), buf((8, 16, 256), BF16),
            buf((64, 1, 128), F32), buf((64, 1, 128), F32),
            buf((2, 128), F32), buf((8, 2, 128), F32),
            buf((256, 256), BF16), buf((256, 256), BF16),
            buf((8, 256, 256), BF16), buf((8, 256, 256), BF16),
            buf((8, 256, 256), BF16), buf((8, 256, 256), BF16),
            pltpu.SemaphoreType.DMA((5,)),
            pltpu.SemaphoreType.REGULAR((2,)), pltpu.SemaphoreType.DMA((8,)),
            pltpu.SemaphoreType.DMA((11,)), pltpu.SemaphoreType.DMA((11,)),
        ],
        compiler_params=pltpu.CompilerParams(
            collective_id=0, has_side_effects=True, vmem_limit_bytes=32 * 2**20
        ),
        name="soft_moe_backward",
    )(*big)
    token_grad, key_grad, in_grad, out_grad = pl.pallas_call(
        write_out,
        out_shape=tuple(pltpu.HBM(shape, kind) for shape, kind in outs),
        in_specs=[any_space] * 4,
        out_specs=(any_space,) * 4,
        scratch_shapes=[pltpu.SemaphoreType.DMA((4,))],
        compiler_params=pltpu.CompilerParams(vmem_limit_bytes=2**20),
        name="write_out",
    )(*held)
    return (token_grad, key_grad.T, in_grad, out_grad)


def solution(mesh):
    return jax.shard_map(
        per_device,
        mesh=mesh,
        in_specs=(
            P("seq", "exp"),
            P("seq", "exp"),
            P(None, "exp"),
            P("exp", None, "seq"),
            P("exp", "seq", None),
        ),
        out_specs=(P("seq", "exp"), P("seq", "exp"), P("exp", None, "seq"), P("exp", "seq", None)),
        check_vma=False,
    )
```

```python
import jax
import jax.numpy as jnp
from jax import lax
from jax.experimental import pallas as pl
from jax.experimental.pallas import tpu as pltpu
from jax.sharding import PartitionSpec as P

MESH = pl.DeviceIdType.MESH
F32, BF16 = jnp.float32, jnp.bfloat16
ROOT_2_PI, CUBE = 0.7978845608, 0.044715
EXP_FAR = ((1, 2), (1, 1), (1, 3), (1, 0), (0, 2), (0, 1), (0, 3))
PAIR_FAR = (4, 3, 5, 2, 6, 1, 7)
MEMBER_FAR = (7, 5, 6, 3, 4, 1, 2)


def dot(lhs, rhs, lhs_dim, rhs_dim):
    return lax.dot_general(
        lhs, rhs, (((lhs_dim,), (rhs_dim,)), ((), ())), preferred_element_type=F32
    )


def kernel(
    keys_hbm, tokens_hbm, cotan_hbm, win_hbm, wout_hbm,
    token_grad_ref, key_ref, in_grad, out_grad,
    key_raw, tok, cot, win, wout,
    key_src, key_buf, log_src, log_buf, c1_src, c1_buf, z_src, z_buf, d_buf,
    e1_src, e1_buf, e2_src, e2_buf, e3_src, e3_buf, g_src, g_buf, h_src, h_buf,
    lse_src, lse_buf, tok_t, cot_t, tok_pair,
    win_by, win_to, wout_by, wout_to,
    load_sem, meet_sem, near_sem, send_sem, recv_sem,
):
    i, e = lax.axis_index("seq"), lax.axis_index("exp")
    x_lo, z, core = i // 32, (i // 2) % 16, i % 2
    pair, own = z // 2, 2 * (x_lo * 2 + core) + z % 2

    def seq_of(member, pair_at):
        return (member // 4) * 32 + (pair_at * 2 + member % 2) * 2 + (member // 2) % 2

    loads = [
        pltpu.make_async_copy(src, dst, load_sem.at[n])
        for n, (src, dst) in enumerate(
            ((keys_hbm, key_raw), (tokens_hbm, tok), (cotan_hbm, cot), (win_hbm, win), (wout_hbm, wout))
        )
    ]
    for load in loads:
        load.start()

    def exp_at(step):
        return (e // 4 + step[0]) % 2 * 4 + (e + step[1]) % 4

    def member(step):
        return (
            (own // 4 + step // 4) % 2 * 4 + (own // 2 + step // 2) % 2 * 2 + (own + step) % 2
        )

    def key_seq(step):
        return (x_lo + step[0]) % 2 * 32 + i % 32

    def signal(sem, seq_at, exp_at):
        pl.semaphore_signal(sem, 1, device_id=(seq_at, exp_at), device_id_type=MESH)

    def meet(step):
        signal(meet_sem.at[step], seq_of(own, (pair + 2**step) % 8), e)
        signal(meet_sem.at[step], seq_of(own, (pair + 8 - 2**step) % 8), e)

    def met(step):
        pl.semaphore_wait(meet_sem.at[step], 2)

    barrier = pltpu.get_barrier_semaphore()
    for step in EXP_FAR:
        signal(barrier, key_seq(step), exp_at(step))
    for step in MEMBER_FAR:
        signal(barrier, seq_of(member(step), pair), e)
    for k in (1, 7):
        signal(barrier, seq_of(own, (pair + k) % 8), e)
    loads[0].wait()
    keys_wide = key_raw[...].astype(F32)
    for k in range(8):
        key_src[k] = keys_wide[:, 256 * k : 256 * k + 256]
    loads[1].wait()
    tok_t[...] = tok[...].T
    pl.semaphore_wait(barrier, 16)

    def send(phase, src, dst, seq_at, exp_at):
        pltpu.make_async_remote_copy(
            src, dst, send_sem.at[phase], recv_sem.at[phase],
            device_id=(seq_at, exp_at), device_id_type=MESH,
        ).start()

    def send_or_keep(phase, here, src, dst, seq_at, exp_at):
        @pl.when(here)
        def _():
            pltpu.make_async_copy(src, dst, recv_sem.at[phase]).start()

        @pl.when(jnp.logical_not(here))
        def _():
            send(phase, src, dst, seq_at, exp_at)

    def arrive(phase, ref):
        pltpu.make_async_copy(ref, ref, recv_sem.at[phase]).wait()

    def send_near(step, src, dst, seq_at, exp_at):
        pltpu.make_async_remote_copy(
            src, dst, send_sem.at[4], near_sem.at[step],
            device_id=(seq_at, exp_at), device_id_type=MESH,
        ).start()

    def arrive_near(step, ref):
        pltpu.make_async_copy(ref, ref, near_sem.at[step]).wait()

    def sent(phase, ref):
        pltpu.make_async_copy(ref, ref, send_sem.at[phase]).wait()

    def sent_some(phase, here, ref, count):
        @pl.when(here)
        def _():
            sent(phase, ref.at[pl.ds(0, count - 1)])

        @pl.when(jnp.logical_not(here))
        def _():
            sent(phase, ref)

    for step in EXP_FAR:
        to = exp_at(step)
        send(0, key_src.at[to], key_buf.at[e], key_seq(step), to)
    meet(0)
    key_buf[e] = key_src[e]
    arrive(0, key_buf.at[pl.ds(0, 7)])
    keys = key_buf[...].reshape(16, 256).astype(BF16)

    log_src[...] = dot(keys, tok_t[...], 1, 0)
    for step in EXP_FAR:
        to = exp_at(step)
        send(1, log_src, log_buf.at[e], i, to)
    met(0)
    meet(1)
    log_buf[e] = log_src[...]
    loads[2].wait()
    arrive(1, log_buf.at[pl.ds(0, 7)])
    logits = log_buf[0]
    for k in range(1, 8):
        logits = logits + log_buf[k]

    peak = jnp.max(logits, axis=1, keepdims=True)
    weight_b = jnp.exp(logits - peak).astype(BF16)
    weight = weight_b.astype(F32)
    total = jnp.sum(weight, axis=1, keepdims=True)
    lse = peak + jnp.log(total)
    row_exp = jnp.exp(logits - jnp.max(logits, axis=0, keepdims=True))
    combine = row_exp / jnp.sum(row_exp, axis=0, keepdims=True)

    slot_part = dot(weight_b, tok[...], 1, 0) / total
    gout_part = dot(combine.astype(BF16), cot[...], 1, 0) * 8.0
    lse_wide = jnp.broadcast_to(lse, (16, 128))
    for b in range(8):
        c1_src[b, 0:2, 0:256] = slot_part[2 * b : 2 * b + 2]
        c1_src[b, 2:4, 0:256] = gout_part[2 * b : 2 * b + 2]
        c1_src[b, 0:2, 256:384] = lse_wide[2 * b : 2 * b + 2]
        c1_src[b, 2:4, 256:384] = jnp.zeros((2, 128), F32)
    home = seq_of(e, pair)
    c1_here = own == e
    for step in EXP_FAR:
        to = exp_at(step)
        send(2, c1_src.at[to], c1_buf.at[own], home, to)
    send_or_keep(2, c1_here, c1_src.at[e], c1_buf.at[own], home, e)
    share = weight / total
    met(1)
    arrive(2, c1_buf)
    def merged(buf):
        top = buf[0, :, 256:384]
        for n in range(1, 8):
            top = jnp.maximum(top, buf[n, :, 256:384])
        norm = jnp.zeros((4, 128), F32)
        low, high = jnp.zeros((4, 128), F32), jnp.zeros((4, 128), F32)
        for n in range(8):
            scale = jnp.exp(buf[n, :, 256:384] - top)
            norm = norm + scale
            low = low + scale * buf[n, :, 0:128]
            high = high + scale * buf[n, :, 128:256]
        return low, high, norm, top + jnp.log(norm)

    row4 = lax.broadcasted_iota(jnp.int32, (4, 256), 0)
    first = row4 < 2
    first_tile = first[:, 0:128]
    low, high, norm, lse_all = merged(c1_buf)
    norm = jnp.where(first_tile, norm, 1.0)
    z_src[:, 0:128] = low / norm
    z_src[:, 128:256] = high / norm
    z_src[:, 256:384] = jnp.where(first_tile, lse_all, 0.0)

    for k in PAIR_FAR:
        send(3, z_src, z_buf.at[pair], seq_of(own, (pair + k) % 8), e)
    z_buf[pair] = z_src[...]
    loads[3].wait()
    loads[4].wait()
    for n in range(8):
        at = n * 256
        pair_in = jnp.concatenate([win[0, at : at + 256, :], win[1, at : at + 256, :]], axis=1)
        win_by[n] = pair_in
        win_to[n] = pair_in.T
        pair_out = wout[:, :, at : at + 256].reshape(256, 256)
        wout_to[n] = pair_out
        wout_by[n] = pair_out.T
    cot_t[...] = cot[...].T
    for n in range(8):
        some = tok[:, 32 * n : 32 * n + 32]
        none = jnp.zeros((256, 32), BF16)
        tok_pair[0:256, 64 * n : 64 * n + 64] = jnp.concatenate([some, none], axis=1)
        tok_pair[256:512, 64 * n : 64 * n + 64] = jnp.concatenate([none, some], axis=1)
    arrive(3, z_buf.at[pl.ds(0, 7)])
    low, high, norm, lse_all = merged(z_buf)
    chunk = jnp.concatenate([low / norm, high / norm], axis=1)

    d_buf[own] = chunk
    for step in MEMBER_FAR:
        send_near(step, d_buf.at[own], d_buf.at[own], seq_of(member(step), pair), e)
    vec = chunk.astype(BF16)
    pre = dot(vec, win_by[own], 1, 0)
    grad_hidden = dot(vec, wout_by[own], 1, 0)
    for step in MEMBER_FAR[::-1]:
        n = member(step)
        arrive_near(step, d_buf.at[n])
        vec = d_buf[n].astype(BF16)
        pre = pre + dot(vec, win_by[n], 1, 0)
        grad_hidden = grad_hidden + dot(vec, wout_by[n], 1, 0)
    pre, grad_hidden = pre[0:2], grad_hidden[2:4]
    tanh = jnp.tanh(ROOT_2_PI * (pre + CUBE * pre * pre * pre))
    hidden = 0.5 * pre * (1.0 + tanh)
    slope = 0.5 * (1.0 + tanh) + 0.5 * pre * (1.0 - tanh * tanh) * ROOT_2_PI * (
        1.0 + 3.0 * CUBE * pre * pre
    )
    lane4 = lax.broadcasted_iota(jnp.int32, (4, 256), 1)
    both = jnp.concatenate([grad_hidden * slope, hidden], axis=0)
    both = jnp.where((lane4 // 128) == (row4 % 2), both, 0.0)
    both_b = both.astype(BF16)

    def partial(n):
        return jnp.where(first, dot(both_b, win_to[n], 1, 0), dot(both_b, wout_to[n], 1, 0))

    for step in MEMBER_FAR:
        to = member(step)
        e1_src[step] = partial(to)
        send(5, e1_src.at[step], e1_buf.at[step], seq_of(to, pair), e)
    full = partial(own)
    arrive(5, e1_buf.at[pl.ds(1, 7)])
    for n in range(1, 8):
        full = full + e1_buf[n]
    e2_src[...] = full
    for k in PAIR_FAR:
        send(6, e2_src, e2_buf.at[pair], seq_of(own, (pair + k) % 8), e)
    e2_buf[pair] = full

    lse_src[...] = lse_all[0:2]
    for step in EXP_FAR:
        send(10, lse_src, lse_buf.at[e], i, exp_at(step))
    lse_buf[e] = lse_all[0:2]
    pre_rows = jnp.where(first, both, 0.0).astype(BF16)
    hid_rows = jnp.where(first, 0.0, both).astype(BF16)
    for n in range(8):
        at = n * 256
        vec = d_buf[n].astype(BF16)
        block = dot(vec, pre_rows, 0, 0).astype(BF16)
        in_grad[0, at : at + 256, :] = block[:, 0:128]
        in_grad[1, at : at + 256, :] = block[:, 128:256]
        block = dot(hid_rows, vec, 0, 0).astype(BF16)
        out_grad[:, :, at : at + 256] = block.reshape(2, 128, 256)

    arrive(10, lse_buf.at[pl.ds(0, 7)])
    lse_rows = lse_buf[...].reshape(16, 128)
    dispatch = share * jnp.exp(lse - jnp.concatenate([lse_rows, lse_rows], axis=1))
    arrive(6, e2_buf.at[pl.ds(0, 7)])
    full = e2_buf[0]
    for n in range(1, 8):
        full = full + e2_buf[n]
    full = full.astype(BF16).astype(F32)
    inner = jnp.sum(full * chunk, axis=1, keepdims=True)
    e3_src[0] = full[0:2]
    e3_src[1] = full[2:4]
    e3_src[2] = jnp.broadcast_to(inner, (4, 256))[0:2]

    for step in MEMBER_FAR:
        send(7, e3_src, e3_buf.at[e], seq_of(member(step), pair), own)
    send_or_keep(7, c1_here, e3_src, e3_buf.at[e], i, own)
    arrive(7, e3_buf)

    def rows_of(kind):
        return e3_buf[:, kind].reshape(16, 256)

    gsi_b = rows_of(0).astype(BF16)
    grad_combine = dot(rows_of(1).astype(BF16), cot_t[...], 1, 0)
    grad_dispatch = dot(gsi_b, tok_t[...], 1, 0) - rows_of(2)
    combine_row = jnp.sum(combine * grad_combine, axis=0, keepdims=True)
    grad_part = dispatch * grad_dispatch + combine * (grad_combine - combine_row)
    grad_part = grad_part.astype(BF16)
    g_src[...] = grad_part
    for step in EXP_FAR:
        send(8, g_src, g_buf.at[e], i, exp_at(step))
    g_buf[e] = grad_part
    arrive(8, g_buf.at[pl.ds(0, 7)])
    grads = g_buf[0].astype(F32)
    for k in range(1, 8):
        grads = grads + g_buf[k].astype(F32)
    grad_logits_b = grads.astype(BF16)

    both_slots = jnp.concatenate([grads, pltpu.roll(grads, 15, 0)], axis=1).astype(BF16)
    rows = dot(both_slots, tok_pair[...], 1, 0)
    for b in range(8):
        for n in range(4):
            h_src[n * 8 + b] = rows[2 * b : 2 * b + 1, 128 * n : 128 * n + 128]
    h_here = i // 8 == e
    for step in EXP_FAR + ((0, 0),):
        b = exp_at(step)
        for k in list(range(1, 8)) + [0]:
            a = (i + k) % 8
            if k == 0 and step == (0, 0):
                send_or_keep(9, h_here, h_src.at[a // 2 * 8 + b], h_buf.at[i], 8 * e + a, b)
            else:
                send(9, h_src.at[a // 2 * 8 + b], h_buf.at[i], 8 * e + a, b)

    left = jnp.concatenate([dispatch.astype(BF16), grad_logits_b], axis=0)
    right = jnp.concatenate([gsi_b, keys], axis=0)
    token_grad_ref[...] = dot(left, right, 0, 0).astype(BF16)
    arrive(9, h_buf)
    rows = h_buf[0]
    for n in range(1, 64):
        rows = rows + h_buf[n]
    rows = jnp.where(i % 2 == 0, rows[:, 0:64], rows[:, 64:128])
    key_ref[...] = jnp.concatenate([rows[:, 0:32], rows[:, 32:64]], axis=0)

    sent(0, key_buf.at[pl.ds(0, 7)])
    sent(1, log_buf.at[pl.ds(0, 7)])
    sent_some(2, c1_here, c1_src, 8)
    sent(3, z_buf.at[pl.ds(0, 7)])
    sent(4, d_buf.at[pl.ds(0, 7)])
    sent(5, e1_buf.at[pl.ds(0, 7)])
    sent(6, e2_buf.at[pl.ds(0, 7)])
    sent_some(7, c1_here, e3_buf, 8)
    sent(8, g_buf.at[pl.ds(0, 7)])
    sent_some(9, h_here, h_buf, 64)
    sent(10, lse_buf.at[pl.ds(0, 7)])


def write_out(*refs):
    sems = refs[-1]
    count = (len(refs) - 1) // 2
    copies = [
        pltpu.make_async_copy(refs[n], refs[count + n], sems.at[n]) for n in range(count)
    ]
    for copy in copies:
        copy.start()
    for copy in copies:
        copy.wait()


def per_device(tokens, cotangent, slot_keys, expert_in, expert_out):
    any_space = pl.BlockSpec(memory_space=pl.ANY)
    buf = pltpu.VMEM
    outs = (
        ((256, 256), BF16), ((2, 32), F32), ((2, 2048, 128), BF16), ((2, 128, 2048), BF16)
    )
    big = [
        pltpu.with_memory_space_constraint(value, pltpu.HBM)
        for value in (slot_keys.T, tokens, cotangent, expert_in, expert_out)
    ]
    held = pl.pallas_call(
        kernel,
        out_shape=tuple(pltpu.VMEM(shape, kind) for shape, kind in outs),
        in_specs=[any_space] * 5,
        scratch_shapes=[
            buf((2, 2048), BF16), buf((256, 256), BF16), buf((256, 256), BF16),
            buf((2, 2048, 128), BF16), buf((2, 128, 2048), BF16),
            buf((8, 2, 256), F32), buf((8, 2, 256), F32),
            buf((16, 256), F32), buf((8, 16, 256), F32),
            buf((8, 4, 384), F32), buf((8, 4, 384), F32),
            buf((4, 384), F32), buf((8, 4, 384), F32),
            buf((8, 4, 256), F32),
            buf((8, 4, 256), F32), buf((8, 4, 256), F32),
            buf((4, 256), F32), buf((8, 4, 256), F32),
            buf((3, 2, 256), F32), buf((8, 3, 2, 256), F32),
            buf((16, 256), BF16), buf((8, 16, 256), BF16),
            buf((32, 1, 128), F32), buf((64, 1, 128), F32),
            buf((2, 128), F32), buf((8, 2, 128), F32),
            buf((256, 256), BF16), buf((256, 256), BF16), buf((512, 512), BF16),
            buf((8, 256, 256), BF16), buf((8, 256, 256), BF16),
            buf((8, 256, 256), BF16), buf((8, 256, 256), BF16),
            pltpu.SemaphoreType.DMA((5,)),
            pltpu.SemaphoreType.REGULAR((2,)), pltpu.SemaphoreType.DMA((8,)),
            pltpu.SemaphoreType.DMA((11,)), pltpu.SemaphoreType.DMA((11,)),
        ],
        compiler_params=pltpu.CompilerParams(
            collective_id=0, has_side_effects=True, vmem_limit_bytes=32 * 2**20
        ),
        name="soft_moe_backward",
    )(*big)
    token_grad, key_grad, in_grad, out_grad = pl.pallas_call(
        write_out,
        out_shape=tuple(pltpu.HBM(shape, kind) for shape, kind in outs),
        in_specs=[any_space] * 4,
        out_specs=(any_space,) * 4,
        scratch_shapes=[pltpu.SemaphoreType.DMA((4,))],
        compiler_params=pltpu.CompilerParams(vmem_limit_bytes=2**20),
        name="write_out",
    )(*held)
    return (token_grad, key_grad.T, in_grad, out_grad)


def solution(mesh):
    return jax.shard_map(
        per_device,
        mesh=mesh,
        in_specs=(
            P("seq", "exp"),
            P("seq", "exp"),
            P(None, "exp"),
            P("exp", None, "seq"),
            P("exp", "seq", None),
        ),
        out_specs=(P("seq", "exp"), P("seq", "exp"), P("exp", None, "seq"), P("exp", "seq", None)),
        check_vma=False,
    )
```

```python
import jax
import jax.numpy as jnp
from jax import lax
from jax.experimental import pallas as pl
from jax.experimental.pallas import tpu as pltpu
from jax.sharding import PartitionSpec as P

MESH = pl.DeviceIdType.MESH
F32, BF16 = jnp.float32, jnp.bfloat16
ROOT_2_PI, CUBE = 0.7978845608, 0.044715
EXP_FAR = ((1, 2), (1, 1), (1, 3), (1, 0), (0, 2), (0, 1), (0, 3))
PAIR_FAR = (4, 3, 5, 2, 6, 1, 7)
MEMBER_FAR = (7, 5, 6, 3, 4, 1, 2)
QUAD_FAR = (3, 2, 1)
PLANE_FAR = (8, 7, 9, 6, 10, 5, 11, 4, 12, 3, 13, 2, 14, 1, 15)


def dot(lhs, rhs, lhs_dim, rhs_dim):
    return lax.dot_general(
        lhs, rhs, (((lhs_dim,), (rhs_dim,)), ((), ())), preferred_element_type=F32
    )


def kernel(
    keys_hbm, tokens_hbm, cotan_hbm, win_hbm, wout_hbm,
    token_grad_ref, key_ref, in_grad, out_grad,
    key_raw, tok, cot, win, wout,
    key_src, key_buf, log_src, log_buf, c1_src, c1_buf, z_src, z_buf, d_buf,
    e1_src, e1_buf, e2_src, e2_buf, e3_src, e3_buf, g_src, g_buf, h_src, h_buf,
    lse_src, lse_buf, tok_t, cot_t, tok_pair,
    w_by, w_to,
    load_sem, meet_sem, near_sem, send_sem, recv_sem,
):
    i, e = lax.axis_index("seq"), lax.axis_index("exp")
    x_lo, z, core = i // 32, (i // 2) % 16, i % 2
    pair, own = z // 2, 2 * (x_lo * 2 + core) + z % 2

    def seq_of(member, pair_at):
        return (member // 4) * 32 + (pair_at * 2 + member % 2) * 2 + (member // 2) % 2

    quad = own // 2

    def plane_seq(quarter, z_at):
        return quarter // 2 * 32 + z_at * 2 + quarter % 2

    def quarter(step):
        return (quad // 2 + step // 2) % 2 * 2 + (quad + step) % 2

    def exp_at(step):
        return (e // 4 + step[0]) % 2 * 4 + (e + step[1]) % 4

    def member(step):
        return (
            (own // 4 + step // 4) % 2 * 4 + (own // 2 + step // 2) % 2 * 2 + (own + step) % 2
        )

    def key_seq(step):
        return (x_lo + step[0]) % 2 * 32 + i % 32

    def signal(sem, seq_at, exp_at):
        pl.semaphore_signal(sem, 1, device_id=(seq_at, exp_at), device_id_type=MESH)

    def meet(step):
        signal(meet_sem.at[step], seq_of(own, (pair + 2**step) % 8), e)
        signal(meet_sem.at[step], seq_of(own, (pair + 8 - 2**step) % 8), e)

    def met(step):
        pl.semaphore_wait(meet_sem.at[step], 2)

    barrier = pltpu.get_barrier_semaphore()
    for step in EXP_FAR:
        signal(barrier, key_seq(step), exp_at(step))
    for step in MEMBER_FAR:
        signal(barrier, seq_of(member(step), pair), e)
    for k in (1, 7):
        signal(barrier, seq_of(own, (pair + k) % 8), e)
    loads = [
        pltpu.make_async_copy(src, dst, load_sem.at[n])
        for n, (src, dst) in enumerate(
            ((keys_hbm, key_raw), (tokens_hbm, tok), (cotan_hbm, cot), (win_hbm, win), (wout_hbm, wout))
        )
    ]
    for load in loads:
        load.start()
    loads[0].wait()
    keys_wide = key_raw[...].astype(F32)
    for k in range(8):
        key_src[k] = keys_wide[:, 256 * k : 256 * k + 256]
    loads[1].wait()
    tok_t[...] = tok[...].T
    pl.semaphore_wait(barrier, 16)

    def send(phase, src, dst, seq_at, exp_at):
        pltpu.make_async_remote_copy(
            src, dst, send_sem.at[phase], recv_sem.at[phase],
            device_id=(seq_at, exp_at), device_id_type=MESH,
        ).start()

    def send_or_keep(phase, here, src, dst, seq_at, exp_at):
        @pl.when(here)
        def _():
            pltpu.make_async_copy(src, dst, recv_sem.at[phase]).start()

        @pl.when(jnp.logical_not(here))
        def _():
            send(phase, src, dst, seq_at, exp_at)

    def arrive(phase, ref):
        pltpu.make_async_copy(ref, ref, recv_sem.at[phase]).wait()

    def send_near(step, src, dst, seq_at, exp_at):
        pltpu.make_async_remote_copy(
            src, dst, send_sem.at[4], near_sem.at[step],
            device_id=(seq_at, exp_at), device_id_type=MESH,
        ).start()

    def arrive_near(step, ref):
        pltpu.make_async_copy(ref, ref, near_sem.at[step]).wait()

    def sent(phase, ref):
        pltpu.make_async_copy(ref, ref, send_sem.at[phase]).wait()

    def sent_some(phase, here, ref, count):
        @pl.when(here)
        def _():
            sent(phase, ref.at[pl.ds(0, count - 1)])

        @pl.when(jnp.logical_not(here))
        def _():
            sent(phase, ref)

    for step in EXP_FAR:
        to = exp_at(step)
        send(0, key_src.at[to], key_buf.at[e], key_seq(step), to)
    meet(0)
    key_buf[e] = key_src[e]
    arrive(0, key_buf.at[pl.ds(0, 7)])
    keys = key_buf[...].reshape(16, 256).astype(BF16)

    log_src[...] = dot(keys, tok_t[...], 1, 0)
    for step in EXP_FAR:
        to = exp_at(step)
        send(1, log_src, log_buf.at[e], i, to)
    met(0)
    meet(1)
    log_buf[e] = log_src[...]
    loads[2].wait()
    arrive(1, log_buf.at[pl.ds(0, 7)])
    logits = log_buf[0]
    for k in range(1, 8):
        logits = logits + log_buf[k]

    peak = jnp.max(logits, axis=1, keepdims=True)
    weight_b = jnp.exp(logits - peak).astype(BF16)
    weight = weight_b.astype(F32)
    total = jnp.sum(weight, axis=1, keepdims=True)
    lse = peak + jnp.log(total)
    row_exp = jnp.exp(logits - jnp.max(logits, axis=0, keepdims=True))
    combine = row_exp / jnp.sum(row_exp, axis=0, keepdims=True)

    slot_part = dot(weight_b, tok[...], 1, 0) / total
    gout_part = dot(combine.astype(BF16), cot[...], 1, 0) * 8.0
    lse_wide = jnp.broadcast_to(lse, (16, 128))
    for b in range(8):
        c1_src[b, 0:2, 0:256] = slot_part[2 * b : 2 * b + 2]
        c1_src[b, 2:4, 0:256] = gout_part[2 * b : 2 * b + 2]
        c1_src[b, 0:2, 256:384] = lse_wide[2 * b : 2 * b + 2]
        c1_src[b, 2:4, 256:384] = jnp.zeros((2, 128), F32)
    home = seq_of(e, pair)
    c1_here = own == e
    for step in EXP_FAR:
        to = exp_at(step)
        send(2, c1_src.at[to], c1_buf.at[own], home, to)
    send_or_keep(2, c1_here, c1_src.at[e], c1_buf.at[own], home, e)
    share = weight / total
    met(1)
    arrive(2, c1_buf)
    def merged(buf):
        top = buf[0, :, 256:384]
        for n in range(1, 8):
            top = jnp.maximum(top, buf[n, :, 256:384])
        norm = jnp.zeros((4, 128), F32)
        low, high = jnp.zeros((4, 128), F32), jnp.zeros((4, 128), F32)
        for n in range(8):
            scale = jnp.exp(buf[n, :, 256:384] - top)
            norm = norm + scale
            low = low + scale * buf[n, :, 0:128]
            high = high + scale * buf[n, :, 128:256]
        return low, high, norm, top + jnp.log(norm)

    row4 = lax.broadcasted_iota(jnp.int32, (4, 256), 0)
    first = row4 < 2
    first_tile = first[:, 0:128]
    low, high, norm, lse_all = merged(c1_buf)
    norm = jnp.where(first_tile, norm, 1.0)
    z_src[:, 0:128] = low / norm
    z_src[:, 128:256] = high / norm
    z_src[:, 256:384] = jnp.where(first_tile, lse_all, 0.0)

    for k in PAIR_FAR:
        send(3, z_src, z_buf.at[pair], seq_of(own, (pair + k) % 8), e)
    z_buf[pair] = z_src[...]
    loads[3].wait()
    loads[4].wait()
    @pl.loop(0, 8)
    def _(n):
        at = pl.ds(pl.multiple_of(n * 256, 256), 256)
        pair_in = jnp.concatenate([win[0, at, :], win[1, at, :]], axis=1)
        pair_out = wout[:, :, at].reshape(256, 256)
        w_by[n, :, 0:256] = pair_in
        w_by[n, :, 256:512] = pair_out.T
        w_to[n, 0:256, :] = pair_in.T
        w_to[n, 256:512, :] = pair_out

    cot_t[...] = cot[...].T
    for n in range(8):
        some = tok[:, 32 * n : 32 * n + 32]
        none = jnp.zeros((256, 32), BF16)
        tok_pair[0:256, 64 * n : 64 * n + 64] = jnp.concatenate([some, none], axis=1)
        tok_pair[256:512, 64 * n : 64 * n + 64] = jnp.concatenate([none, some], axis=1)
    arrive(3, z_buf.at[pl.ds(0, 7)])
    low, high, norm, lse_all = merged(z_buf)
    chunk = jnp.concatenate([low / norm, high / norm], axis=1)

    d_buf[own] = chunk
    for step in MEMBER_FAR:
        send_near(step, d_buf.at[own], d_buf.at[own], seq_of(member(step), pair), e)
    vec = chunk.astype(BF16)
    wide = dot(vec, w_by[own], 1, 0)
    for step in MEMBER_FAR[::-1]:
        n = member(step)
        arrive_near(step, d_buf.at[n])
        vec = d_buf[n].astype(BF16)
        wide = wide + dot(vec, w_by[n], 1, 0)
    pre, grad_hidden = wide[0:2, 0:256], wide[2:4, 256:512]
    tanh = jnp.tanh(ROOT_2_PI * (pre + CUBE * pre * pre * pre))
    hidden = 0.5 * pre * (1.0 + tanh)
    slope = 0.5 * (1.0 + tanh) + 0.5 * pre * (1.0 - tanh * tanh) * ROOT_2_PI * (
        1.0 + 3.0 * CUBE * pre * pre
    )
    lane4 = lax.broadcasted_iota(jnp.int32, (4, 256), 1)
    both = jnp.concatenate([grad_hidden * slope, hidden], axis=0)
    both = jnp.where((lane4 // 128) == (row4 % 2), both, 0.0)
    pre_rows = jnp.where(first, both, 0.0).astype(BF16)
    hid_rows = jnp.where(first, 0.0, both).astype(BF16)
    rows_wide = jnp.concatenate([pre_rows, hid_rows], axis=1)

    def partial(n):
        return dot(rows_wide, w_to[n], 1, 0)

    for step in QUAD_FAR:
        to = quarter(step)
        for h in range(2):
            e1_src[step, h] = partial(2 * to + h)
        send(5, e1_src.at[step], e1_buf.at[step], plane_seq(to, z), e)
    full = [partial(2 * quad + h) for h in range(2)]
    arrive(5, e1_buf.at[pl.ds(1, 3)])
    packed = []
    for h in range(2):
        some = full[h] + e1_buf[1, h] + (e1_buf[2, h] + e1_buf[3, h])
        packed += [some[:, 0:128], some[:, 128:256]]
    packed = jnp.concatenate(packed, axis=0).astype(BF16)
    e2_src[...] = packed
    for k in PLANE_FAR:
        send(6, e2_src, e2_buf.at[z], plane_seq(quad, (z + k) % 16), e)
    e2_buf[z] = packed

    lse_src[...] = lse_all[0:2]
    for step in EXP_FAR:
        send(10, lse_src, lse_buf.at[e], i, exp_at(step))
    lse_buf[e] = lse_all[0:2]
    @pl.loop(0, 8)
    def _(n):
        at = pl.ds(pl.multiple_of(n * 256, 256), 256)
        vec = d_buf[n].astype(BF16)
        block = dot(vec, pre_rows, 0, 0).astype(BF16)
        in_grad[0, at, :] = block[:, 0:128]
        in_grad[1, at, :] = block[:, 128:256]
        block = dot(hid_rows, vec, 0, 0).astype(BF16)
        out_grad[:, :, at] = block.reshape(2, 128, 256)

    arrive(10, lse_buf.at[pl.ds(0, 7)])
    lse_rows = lse_buf[...].reshape(16, 128)
    dispatch = share * jnp.exp(lse - jnp.concatenate([lse_rows, lse_rows], axis=1))
    arrive(6, e2_buf.at[pl.ds(0, 15)])
    sums = [e2_buf[n].astype(F32) for n in range(16)]
    while len(sums) > 1:
        sums = [sums[n] + sums[n + 1] for n in range(0, len(sums), 2)]
    packed = sums[0].astype(BF16).astype(F32)
    for h in range(2):
        full = jnp.concatenate([packed[8 * h : 8 * h + 4], packed[8 * h + 4 : 8 * h + 8]], axis=1)
        inner = jnp.sum(full * d_buf[2 * quad + h], axis=1, keepdims=True)
        e3_src[h, 0] = full[0:2]
        e3_src[h, 1] = full[2:4]
        e3_src[h, 2] = jnp.broadcast_to(inner, (4, 256))[0:2]

    for step in QUAD_FAR:
        for h in range(2):
            send(7, e3_src.at[h], e3_buf.at[e], plane_seq(quarter(step), z), 2 * quad + h)
    for h in range(2):
        send_or_keep(7, 2 * quad + h == e, e3_src.at[h], e3_buf.at[e], i, 2 * quad + h)
    arrive(7, e3_buf)

    def rows_of(kind):
        return e3_buf[:, kind].reshape(16, 256)

    gsi_b = rows_of(0).astype(BF16)
    grad_combine = dot(rows_of(1).astype(BF16), cot_t[...], 1, 0)
    grad_dispatch = dot(gsi_b, tok_t[...], 1, 0) - rows_of(2)
    combine_row = jnp.sum(combine * grad_combine, axis=0, keepdims=True)
    grad_part = dispatch * grad_dispatch + combine * (grad_combine - combine_row)
    grad_part = grad_part.astype(BF16)
    g_src[...] = grad_part
    for step in EXP_FAR:
        send(8, g_src, g_buf.at[e], i, exp_at(step))
    g_buf[e] = grad_part
    arrive(8, g_buf.at[pl.ds(0, 7)])
    grads = g_buf[0].astype(F32)
    for k in range(1, 8):
        grads = grads + g_buf[k].astype(F32)
    grad_logits_b = grads.astype(BF16)

    both_slots = jnp.concatenate([grads, pltpu.roll(grads, 15, 0)], axis=1).astype(BF16)
    rows = dot(both_slots, tok_pair[...], 1, 0)
    for b in range(8):
        for n in range(4):
            h_src[n * 8 + b] = rows[2 * b : 2 * b + 1, 128 * n : 128 * n + 128]
    h_here = i // 8 == e
    for step in EXP_FAR + ((0, 0),):
        b = exp_at(step)
        for k in list(range(1, 8)) + [0]:
            a = (i + k) % 8
            if k == 0 and step == (0, 0):
                send_or_keep(9, h_here, h_src.at[a // 2 * 8 + b], h_buf.at[i], 8 * e + a, b)
            else:
                send(9, h_src.at[a // 2 * 8 + b], h_buf.at[i], 8 * e + a, b)

    left = jnp.concatenate([dispatch.astype(BF16), grad_logits_b], axis=0)
    right = jnp.concatenate([gsi_b, keys], axis=0)
    token_grad_ref[...] = dot(left, right, 0, 0).astype(BF16)

    sent(0, key_buf.at[pl.ds(0, 7)])
    sent(1, log_buf.at[pl.ds(0, 7)])
    sent_some(2, c1_here, c1_src, 8)
    sent(3, z_buf.at[pl.ds(0, 7)])
    sent(4, d_buf.at[pl.ds(0, 7)])
    sent(5, e1_buf.at[pl.ds(0, 3)])
    sent(6, e2_buf.at[pl.ds(0, 15)])
    sent_some(7, quad == e // 2, e3_buf, 8)
    sent(8, g_buf.at[pl.ds(0, 7)])
    sent_some(9, h_here, h_buf, 64)
    sent(10, lse_buf.at[pl.ds(0, 7)])
    arrive(9, h_buf)
    sums = [h_buf[n] for n in range(64)]
    while len(sums) > 1:
        sums = [sums[n] + sums[n + 1] for n in range(0, len(sums), 2)]
    rows = sums[0]
    rows = jnp.where(i % 2 == 0, rows[:, 0:64], rows[:, 64:128])
    key_ref[...] = jnp.concatenate([rows[:, 0:32], rows[:, 32:64]], axis=0)


def write_out(*refs):
    sems = refs[-1]
    count = (len(refs) - 1) // 2
    copies = [
        pltpu.make_async_copy(refs[n], refs[count + n], sems.at[n]) for n in range(count)
    ]
    for copy in copies:
        copy.start()
    for copy in copies:
        copy.wait()


def per_device(tokens, cotangent, slot_keys, expert_in, expert_out):
    any_space = pl.BlockSpec(memory_space=pl.ANY)
    buf = pltpu.VMEM
    outs = (
        ((256, 256), BF16), ((2, 32), F32), ((2, 2048, 128), BF16), ((2, 128, 2048), BF16)
    )
    big = [
        pltpu.with_memory_space_constraint(value, pltpu.HBM)
        for value in (slot_keys.T, tokens, cotangent, expert_in, expert_out)
    ]
    held = pl.pallas_call(
        kernel,
        out_shape=tuple(pltpu.VMEM(shape, kind) for shape, kind in outs),
        in_specs=[any_space] * 5,
        scratch_shapes=[
            buf((2, 2048), BF16), buf((256, 256), BF16), buf((256, 256), BF16),
            buf((2, 2048, 128), BF16), buf((2, 128, 2048), BF16),
            buf((8, 2, 256), F32), buf((8, 2, 256), F32),
            buf((16, 256), F32), buf((8, 16, 256), F32),
            buf((8, 4, 384), F32), buf((8, 4, 384), F32),
            buf((4, 384), F32), buf((8, 4, 384), F32),
            buf((8, 4, 256), F32),
            buf((4, 2, 4, 256), F32), buf((4, 2, 4, 256), F32),
            buf((16, 128), BF16), buf((16, 16, 128), BF16),
            buf((2, 3, 2, 256), F32), buf((8, 3, 2, 256), F32),
            buf((16, 256), BF16), buf((8, 16, 256), BF16),
            buf((32, 1, 128), F32), buf((64, 1, 128), F32),
            buf((2, 128), F32), buf((8, 2, 128), F32),
            buf((256, 256), BF16), buf((256, 256), BF16), buf((512, 512), BF16),
            buf((8, 256, 512), BF16), buf((8, 512, 256), BF16),
            pltpu.SemaphoreType.DMA((5,)),
            pltpu.SemaphoreType.REGULAR((2,)), pltpu.SemaphoreType.DMA((8,)),
            pltpu.SemaphoreType.DMA((11,)), pltpu.SemaphoreType.DMA((11,)),
        ],
        compiler_params=pltpu.CompilerParams(
            collective_id=0, has_side_effects=True, vmem_limit_bytes=32 * 2**20
        ),
        name="soft_moe_backward",
    )(*big)
    token_grad, key_grad, in_grad, out_grad = pl.pallas_call(
        write_out,
        out_shape=tuple(pltpu.HBM(shape, kind) for shape, kind in outs),
        in_specs=[any_space] * 4,
        out_specs=(any_space,) * 4,
        scratch_shapes=[pltpu.SemaphoreType.DMA((4,))],
        compiler_params=pltpu.CompilerParams(vmem_limit_bytes=2**20),
        name="write_out",
    )(*held)
    return (token_grad, key_grad.T, in_grad, out_grad)


def solution(mesh):
    return jax.shard_map(
        per_device,
        mesh=mesh,
        in_specs=(
            P("seq", "exp"),
            P("seq", "exp"),
            P(None, "exp"),
            P("exp", None, "seq"),
            P("exp", "seq", None),
        ),
        out_specs=(P("seq", "exp"), P("seq", "exp"), P("exp", None, "seq"), P("exp", "seq", None)),
        check_vma=False,
    )
```
